512 devices in a mesh: bucket: 128 (over x, y, z_lo, core), rep: 4 (over z_hi).
Axes of the slice: x: 4, y: 8, z: 8 (z_hi: 4, z_lo: 2; z = z_hi * 2 + z_lo), core: 2. Of those that a mesh axis runs over, the one named last changes fastest.
Arguments:
- src_table: float32 [262144, 256], P(('bucket', 'rep')), may hold values from -6 to 6
- src_state: float32 [262144], P(('bucket', 'rep')), may hold values from 0.05 to 0.5
- dst_table: float32 [65536, 256], P(('bucket', 'rep')), may hold values from -6 to 6
- dst_state: float32 [65536], P(('bucket', 'rep')), may hold values from 0.05 to 0.5
- rel_table: float32 [64, 256], replicated, may hold values from 0.25 to 1.75
- partners: int32 [2, 128], replicated, may hold values from 0 to 127, as said below
- tiles: int32 [128, 4, 2, 64], P('bucket', 'rep'), may hold values from 0 to 15
- tile_rel: int32 [128, 4, 2, 64], P('bucket', 'rep'), may hold values from 0 to 63
- counts: int32 [128, 4, 2], P('bucket', 'rep'), may hold values from 1 to 64, as said below
Outputs:
- src_out: float32 [262144, 256], P(('bucket', 'rep'))
- src_state_out: float32 [262144], P(('bucket', 'rep'))
- dst_out: float32 [65536, 256], P(('bucket', 'rep'))
- dst_state_out: float32 [65536], P(('bucket', 'rep'))
The draws below stay inside these ranges and needn't reach their ends.
Inputs may be any that keep to these rules, and one draw needn't show every extreme that they name: partners[k, b] = b XOR m_k for one mask m_k of round k, 1 to 127, a different mask in each round. Only the first counts[b, r, k] slots of a device's round are live; some device holds 64 live tiles in every draw.
All inputs are finite; a program needn't handle non-finite values.
Results may differ from the reference program's by a relative error of at most 0.002.
Values may be sent and summed in bfloat16 or wider, within the bound.
A program may use at most 64 MiB of HBM per device.

```python
import math
import jax
import jax.numpy as jnp
from jax import lax

D = 256
TILE = 128
ROUNDS = 2
REL = 64
SRC_DEV = 512
MAXT = 64
PART = 512
ENT_SRC = 262144
ENT_DST = 65536
N_BUCKET = 128
N_REP = 4


def draw_partners(key, part):
    order = jax.random.permutation(jax.random.fold_in(key, 21), N_BUCKET - 1) + 1
    masks = order[:ROUNDS].astype(jnp.int32)
    buckets = jnp.arange(N_BUCKET, dtype=jnp.int32)
    return jnp.bitwise_xor(buckets[None, :], masks[:, None]).astype(jnp.int32)


def draw_counts(key, part):
    shape = (N_BUCKET, N_REP, ROUNDS)
    base = jax.random.randint(jax.random.fold_in(key, 11), shape, 1, MAXT // 2 + 1)
    filled = jax.random.randint(jax.random.fold_in(key, 12), shape, 0, 8) == 0
    values = jnp.where(filled, MAXT, base).reshape(-1)
    where_full = jax.random.randint(jax.random.fold_in(key, 13), (), 0, values.shape[0])
    values = values.at[where_full].set(MAXT)
    return values.reshape(shape).astype(jnp.int32)


def touch_ends(values, rng, least, high):
    index_at = [jax.random.randint(jax.random.fold_in(rng, axis), (), 0, length) for axis, length in enumerate(values.shape)]
    main_axis = values.shape.index(max(values.shape))
    beside = index_at[:main_axis] + [(index_at[main_axis] + 1) % values.shape[main_axis]] + index_at[main_axis + 1:]
    return values.at[tuple(index_at)].set(least).at[tuple(beside)].set(high)


def block_levels(stream_key, dims, shards, low, high):
    level, own = 1.0, jax.random.fold_in(stream_key, 6)
    for position, parts in shards:
        heights = jnp.exp(jax.random.uniform(jax.random.fold_in(own, position), (parts,), jnp.float32, low / len(shards), high / len(shards)))
        level = level * jnp.repeat(heights, dims[position] // parts).reshape([-1 if axis == position else 1 for axis in range(len(dims))])
    return level


def centred(own_key, shape, width, most, pieces=(), kind=jnp.bfloat16):
    loudness = block_levels(own_key, shape, pieces, -0.22, 0.18) if pieces else 1.0
    drawn = jax.random.normal(own_key, shape, jnp.float32) * width * loudness
    return jnp.minimum(jnp.maximum(drawn, -most), most).astype(kind)


def setup_inputs(seed: int = 0) -> dict:
    key_of = jax.random.split(jax.random.key(seed), 10)
    src_table = centred(key_of[0], (ENT_SRC, D), 1.0, 6.0, ((0, 512),), jnp.float32)
    src_state = jnp.clip(jnp.exp(math.log(0.5) - 2.3025851 * jax.random.uniform(key_of[1], (ENT_SRC,), jnp.float32) ** block_levels(key_of[1], (ENT_SRC,), ((0, 512),), -0.2, 0.2)), 0.05, 0.5)
    dst_table = centred(key_of[2], (ENT_DST, D), 1.0, 6.0, ((0, 512),), jnp.float32)
    dst_state = jnp.clip(jnp.exp(math.log(0.5) - 2.3025851 * jax.random.uniform(key_of[3], (ENT_DST,), jnp.float32) ** block_levels(key_of[3], (ENT_DST,), ((0, 512),), -0.2, 0.2)), 0.05, 0.5)
    rel_table = jnp.clip(jax.random.uniform(key_of[4], (REL, D), jnp.float32, 0.25, 1.75), 0.25, 1.75)
    partners = draw_partners(jax.random.fold_in(key_of[9], 71), 0)
    tiles = touch_ends(jax.random.randint(key_of[6], (N_BUCKET, N_REP, ROUNDS, MAXT), 0, SRC_DEV // TILE * (PART // TILE)), jax.random.fold_in(key_of[6], 1), 0, (SRC_DEV // TILE * (PART // TILE)) - 1).astype(jnp.int32)
    tile_rel = touch_ends(jax.random.randint(key_of[7], (N_BUCKET, N_REP, ROUNDS, MAXT), 0, REL), jax.random.fold_in(key_of[7], 1), 0, REL - 1).astype(jnp.int32)
    counts = draw_counts(jax.random.fold_in(key_of[9], 71), 0)
    return dict(src_table=src_table, src_state=src_state, dst_table=dst_table, dst_state=dst_state, rel_table=rel_table, partners=partners, tiles=tiles, tile_rel=tile_rel, counts=counts)


learn_rate = 0.1

def tile_terms(src_blocks, dst_blocks, tile_list, rel_list, live_count, rel_table):
    dst_number = dst_blocks.shape[0]
    src_number = src_blocks.shape[0]
    score_scale = D ** (-0.5)
    src_index = (tile_list // dst_number).astype(jnp.int32)
    dst_index = (tile_list % dst_number).astype(jnp.int32)
    rel_pick = rel_table[rel_list.astype(jnp.int32)]
    src_pick = src_blocks[src_index].astype(jnp.float32)
    dst_pick = dst_blocks[dst_index].astype(jnp.float32)
    src_rel = (src_pick * rel_pick[:, None, :]).astype(jnp.bfloat16)
    src_rel = lax.optimization_barrier(src_rel).astype(jnp.float32)
    scores = jnp.einsum('tnd,tmd->tnm', src_rel, dst_pick, precision=lax.Precision.HIGHEST) * score_scale
    live_tiles = (jnp.arange(MAXT, dtype=jnp.int32) < live_count).astype(jnp.float32)
    diagonal_ones = jnp.eye(TILE, dtype=jnp.float32)
    slope = ((jax.nn.sigmoid(scores) - diagonal_ones) * live_tiles[:, None, None]).astype(jnp.bfloat16)
    slope = lax.optimization_barrier(slope).astype(jnp.float32)
    src_terms = jnp.einsum('tnm,tmd->tnd', slope, dst_pick, precision=lax.Precision.HIGHEST) * rel_pick[:, None, :] * score_scale
    dst_terms = jnp.einsum('tnm,tnd->tmd', slope, src_rel, precision=lax.Precision.HIGHEST) * score_scale
    src_onehot = (src_index[:, None] == jnp.arange(src_number, dtype=jnp.int32)[None, :]).astype(jnp.float32)
    dst_onehot = (dst_index[:, None] == jnp.arange(dst_number, dtype=jnp.int32)[None, :]).astype(jnp.float32)
    src_grad = jnp.einsum('ts,tnd->snd', src_onehot, src_terms, precision=lax.Precision.HIGHEST)
    dst_grad = jnp.einsum('ts,tnd->snd', dst_onehot, dst_terms, precision=lax.Precision.HIGHEST)
    return (src_grad.reshape(-1, D), dst_grad.reshape(-1, D))

def adagrad(embedding, accumulator, gradient):
    accumulator = accumulator + lax.optimization_barrier(jnp.mean(gradient * gradient, axis=1))
    embedding = embedding - learn_rate * gradient / jnp.sqrt(accumulator)[:, None]
    return (embedding, accumulator)

def reference(src_table, src_state, dst_table, dst_state, rel_table, partners, tiles, tile_rel, counts):
    for round_index in range(ROUNDS):
        src_low = src_table.astype(jnp.bfloat16).reshape(N_BUCKET, N_REP, SRC_DEV // TILE, TILE, D)
        dst_low = dst_table.astype(jnp.bfloat16).reshape(N_BUCKET, PART // TILE, TILE, D)
        partner_row = partners[round_index]

        def one_bucket(inputs):
            src_bucket, partner_bucket, tiles_bucket, rel_bucket, counts_bucket = inputs
            dst_bucket = dst_low[partner_bucket]
            src_grad, dst_part = jax.vmap(tile_terms, in_axes=(0, None, 0, 0, 0, None))(src_bucket, dst_bucket, tiles_bucket, rel_bucket, counts_bucket, rel_table)
            dst_part = lax.optimization_barrier(dst_part.astype(jnp.bfloat16)).astype(jnp.float32)
            return (src_grad, lax.optimization_barrier(jnp.sum(dst_part, axis=0)).astype(jnp.bfloat16))
        src_grad, dst_sum = lax.map(one_bucket, (src_low, partner_row, tiles[:, :, round_index], tile_rel[:, :, round_index], counts[:, :, round_index]))
        dst_grad = dst_sum[partner_row].astype(jnp.float32).reshape(-1, D)
        src_table, src_state = adagrad(src_table, src_state, src_grad.reshape(-1, D))
        dst_table, dst_state = adagrad(dst_table, dst_state, dst_grad)
    return (src_table, src_state, dst_table, dst_state)
```

```python
import jax
import jax.numpy as jnp
from jax import lax
from jax.experimental import pallas as pl
from jax.experimental.pallas import tpu as pltpu
from jax.sharding import PartitionSpec as P

D = 256
TILE = 128
ROUNDS = 2


learn_rate = 0.1


def partner(array, axis, bit):
    return lax.ppermute(array, axis, [(i, i ^ 1 << bit) for i in range(lax.axis_size(axis))])


def from_everyone(array, axis):
    copies = jnp.broadcast_to(array, (lax.axis_size(axis), *array.shape))
    return lax.all_to_all(copies, axis, split_axis=0, concat_axis=0, tiled=True)


def joined_along(parts, dim):
    dims = list(parts.shape[1:])
    dims[dim] *= parts.shape[0]
    return jnp.moveaxis(parts, 0, dim).reshape(dims)


def gather_directly(array, axis, dim):
    parts = from_everyone(array, axis)
    return joined_along(parts, dim)


def cut_along(array, dim, length):
    dims = array.shape
    parts = array.reshape(*dims[:dim], length, dims[dim] // length, *dims[dim + 1 :])
    return jnp.moveaxis(parts, dim, 0)


def sum_at_owner(array, axis, dim):
    length = lax.axis_size(axis)
    parts = lax.all_to_all(cut_along(array, dim, length), axis, 0, 0, tiled=True)
    return jnp.sum(parts.astype(jnp.float32), axis=0)


def step_bit(moved, rows, round_mask, bit_number):
    flag = jnp.bitwise_and(jnp.right_shift(round_mask, bit_number), 1) == 1
    return lax.cond(flag, moved, lambda values: values, rows)


def route_slice(rows, round_mask, bit_count):
    for bit_number in range(bit_count):

        def moved(values, bit_number=bit_number):
            return partner(values, "bucket", bit_number)

        rows = step_bit(moved, rows, round_mask, bit_number)
    return rows


def return_slice(rows, round_mask, bit_count):
    for bit_number in range(bit_count):

        def moved(values, bit_number=bit_number):
            return partner(values, "bucket", bit_number)

        rows = step_bit(moved, rows, round_mask, bit_number)
    return rows


UNROLL = 4


def tile_kernel(code_ref, rel_id_ref, count_ref, src_ref, part_ref, rel_ref, src_out, dst_out, src_low):
    src_low[...] = src_ref[...].astype(jnp.bfloat16).astype(jnp.float32)
    src_out[...] = jnp.zeros_like(src_out)
    dst_out[...] = jnp.zeros_like(dst_out)
    live = count_ref[0]
    row = lax.broadcasted_iota(jnp.int32, (TILE, TILE), 0)
    col = lax.broadcasted_iota(jnp.int32, (TILE, TILE), 1)
    shift = jnp.where(row == col, -0.5, 0.5).astype(jnp.float32)

    def step(group, carry):
        for lane in range(UNROLL):
            slot = group * UNROLL + lane
            code = code_ref[slot]
            s = pl.multiple_of((code // 4) * TILE, TILE)
            e = pl.multiple_of((code % 4) * TILE, TILE)
            rel = rel_ref[pl.ds(rel_id_ref[slot], 1), :]
            src_rel = (src_low[pl.ds(s, TILE), :] * rel).astype(jnp.bfloat16)
            dst = part_ref[pl.ds(e, TILE), :]
            scores = lax.dot_general(
                src_rel, dst, (((1,), (1,)), ((), ())), preferred_element_type=jnp.float32
            )
            on = jnp.where(slot < live, 1.0, 0.0).astype(jnp.float32)
            slope = ((jnp.tanh(scores * (0.5 * D**-0.5)) * 0.5 + shift) * on).astype(jnp.bfloat16)
            src_term = jnp.dot(slope, dst, preferred_element_type=jnp.float32)
            dst_term = lax.dot_general(
                slope, src_rel, (((0,), (0,)), ((), ())), preferred_element_type=jnp.float32
            )
            src_out[pl.ds(s, TILE), :] += src_term * rel
            dst_out[pl.ds(e, TILE), :] += dst_term
        return carry

    lax.fori_loop(0, (live + UNROLL - 1) // UNROLL, step, 0)
    src_out[...] = src_out[...] * D**-0.5
    dst_out[...] = dst_out[...] * D**-0.5


def tile_work(src_table, partition, tile_list, rel_list, live_count, rel_table):
    smem = pl.BlockSpec(memory_space=pltpu.SMEM)
    vmem = pl.BlockSpec(memory_space=pltpu.VMEM)
    return pl.pallas_call(
        tile_kernel,
        out_shape=(
            jax.ShapeDtypeStruct(src_table.shape, jnp.float32),
            jax.ShapeDtypeStruct(partition.shape, jnp.float32),
        ),
        in_specs=[smem, smem, smem, vmem, vmem, vmem],
        out_specs=(vmem, vmem),
        scratch_shapes=[pltpu.VMEM(src_table.shape, jnp.float32)],
        compiler_params=pltpu.CompilerParams(vmem_limit_bytes=32 * 2**20),
    )(tile_list, rel_list, live_count, src_table, partition, rel_table)


def adagrad(embedding, accumulator, gradient):
    accumulator = accumulator + jnp.mean(gradient * gradient, axis=1)
    embedding = embedding - learn_rate * gradient / jnp.sqrt(accumulator)[:, None]
    return (embedding, accumulator)


def per_device(
    src_table, src_state, dst_table, dst_state, rel_table, partners, tiles, tile_rel, counts
):
    bit_count = lax.axis_size("bucket").bit_length() - 1
    for round_index in range(ROUNDS):
        round_mask = partners[round_index, 0]
        own_rows = dst_table.astype(jnp.bfloat16)
        moved_rows = route_slice(own_rows, round_mask, bit_count)
        partition = gather_directly(moved_rows, "rep", 0)
        src_grad, dst_part = tile_work(
            src_table,
            partition,
            tiles[0, 0, round_index],
            tile_rel[0, 0, round_index],
            counts[0, 0, round_index : round_index + 1],
            rel_table,
        )
        summed = sum_at_owner(dst_part.astype(jnp.bfloat16), "rep", 0).astype(jnp.bfloat16)
        dst_grad = return_slice(summed, round_mask, bit_count).astype(jnp.float32)
        src_table, src_state = adagrad(src_table, src_state, src_grad)
        dst_table, dst_state = adagrad(dst_table, dst_state, dst_grad)
    return (src_table, src_state, dst_table, dst_state)


def solution(mesh):
    in_specs = (
        P(("bucket", "rep"), None),
        P(("bucket", "rep")),
        P(("bucket", "rep"), None),
        P(("bucket", "rep")),
        P(),
        P(),
        P("bucket", "rep", None, None),
        P("bucket", "rep", None, None),
        P("bucket", "rep", None),
    )
    out_specs = (
        P(("bucket", "rep"), None),
        P(("bucket", "rep")),
        P(("bucket", "rep"), None),
        P(("bucket", "rep")),
    )
    return jax.shard_map(
        per_device, mesh=mesh, in_specs=in_specs, out_specs=out_specs, check_vma=False
    )
```

```python
import functools

import jax
import jax.numpy as jnp
from jax import lax
from jax.experimental import pallas as pl
from jax.experimental.pallas import tpu as pltpu
from jax.sharding import PartitionSpec as P

D = 256
TILE = 128
ROUNDS = 2


learn_rate = 0.1


HALF = TILE // 2
MESH = pl.DeviceIdType.MESH


def paired(mask):
    me = lax.axis_index("bucket")
    other = me
    for bit in range(mask.bit_length()):
        if mask >> bit & 1:
            other = other + (1 << bit) * (1 - 2 * lax.rem(lax.div(me, 1 << bit), 2))
    return other


def around():
    me = lax.axis_index("rep")
    return me, lax.rem(me + 3, 4), lax.rem(me + 1, 4), lax.rem(me + 2, 4)


def greet(devices):
    barrier = pltpu.get_barrier_semaphore()
    for device in devices:
        pl.semaphore_signal(barrier, inc=1, device_id=device, device_id_type=MESH)
    pl.semaphore_wait(barrier, len(devices))


def rows(quarter, half):
    return pl.ds(pl.multiple_of(quarter * TILE + half * HALF, HALF), HALF)


def gather_kernel(mask, table_ref, part_ref, low_ref, send, recv):
    me, left, right, far = around()
    to_left, to_right, to_pair = {"rep": left}, {"rep": right}, {"bucket": paired(mask)}

    def copy(slot, src, dst, device):
        return pltpu.make_async_remote_copy(
            src, dst, send.at[slot], recv.at[slot], device_id=device, device_id_type=MESH
        )

    low_ref[...] = table_ref[...].astype(jnp.bfloat16)
    greet((to_pair, to_left, to_right))
    hop = [
        copy(half, low_ref.at[rows(0, half)], part_ref.at[rows(me, half)], to_pair)
        for half in range(2)
    ]
    hop[0].start()
    hop[1].start()
    own = [part_ref.at[rows(me, half)] for half in range(2)]
    going_right = [copy(2 + half, own[half], own[half], to_right) for half in range(2)]
    going_left = [copy(4 + half, own[half], own[half], to_left) for half in range(2)]
    hop[0].wait_recv()
    going_right[0].start()
    going_left[0].start()
    hop[1].wait_recv()
    going_left[1].start()
    going_right[1].start()
    passed = part_ref.at[rows(left, 0)]
    on_right = copy(6, passed, passed, to_right)
    going_right[0].wait_recv()
    on_right.start()
    passed = part_ref.at[rows(right, 1)]
    on_left = copy(7, passed, passed, to_left)
    going_left[1].wait_recv()
    on_left.start()
    going_left[0].wait_recv()
    going_right[1].wait_recv()
    on_right.wait_recv()
    on_left.wait_recv()
    for sent in (*hop, *going_right, *going_left, on_right, on_left):
        sent.wait_send()


def gathered(mask, collective_id, table):
    vmem = pl.BlockSpec(memory_space=pltpu.VMEM)
    return pl.pallas_call(
        functools.partial(gather_kernel, mask),
        out_shape=jax.ShapeDtypeStruct((4 * TILE, D), jnp.bfloat16),
        in_specs=[vmem],
        out_specs=vmem,
        scratch_shapes=[
            pltpu.VMEM((TILE, D), jnp.bfloat16),
            pltpu.SemaphoreType.DMA((8,)),
            pltpu.SemaphoreType.DMA((8,)),
        ],
        compiler_params=pltpu.CompilerParams(
            collective_id=collective_id, has_side_effects=True, vmem_limit_bytes=16 * 2**20
        ),
    )(table)


def diagonal():
    row = lax.broadcasted_iota(jnp.int32, (TILE, TILE), 0)
    col = lax.broadcasted_iota(jnp.int32, (TILE, TILE), 1)
    return row == col


def adagrad_block(table, state_row, grad, diag):
    mean = jnp.sum(grad * grad, axis=1, keepdims=True) * (1 / D)
    state = jnp.sum(jnp.where(diag, state_row, 0.0), axis=1, keepdims=True) + mean
    table = table - grad * (learn_rate / jnp.sqrt(state))
    return table, jnp.sum(jnp.where(diag, state, 0.0), axis=0, keepdims=True)


def reduce_kernel(
    mask, part_ref, table_ref, state_ref, table_out, state_out, relay, added, side, total, got, send, recv
):
    me, left, right, far = around()
    to_left, to_right, to_pair = {"rep": left}, {"rep": right}, {"bucket": paired(mask)}

    def copy(slot, src, dst, device):
        return pltpu.make_async_remote_copy(
            src, dst, send.at[slot], recv.at[slot], device_id=device, device_id_type=MESH
        )

    def wide(ref):
        return ref[...].astype(jnp.float32)

    greet((to_pair, to_left, to_right))
    first = copy(0, part_ref.at[rows(far, 0)], relay.at[rows(0, 0)], to_left)
    second = copy(1, part_ref.at[rows(far, 1)], relay.at[rows(0, 1)], to_right)
    left_one = copy(2, part_ref.at[rows(left, 1)], side.at[rows(1, 1)], to_left)
    right_zero = copy(3, part_ref.at[rows(right, 0)], side.at[rows(0, 0)], to_right)
    left_zero = copy(4, added.at[rows(0, 0)], side.at[rows(1, 0)], to_left)
    right_one = copy(5, added.at[rows(0, 1)], side.at[rows(0, 1)], to_right)
    back = [copy(6 + half, total.at[rows(0, half)], got.at[rows(0, half)], to_pair) for half in range(2)]
    first.start()
    second.start()
    left_one.start()
    right_zero.start()
    first.wait_recv()
    added[rows(0, 0), :] = (
        wide(relay.at[rows(0, 0)]) + wide(part_ref.at[rows(left, 0)])
    ).astype(jnp.bfloat16)
    left_zero.start()
    second.wait_recv()
    added[rows(0, 1), :] = (
        wide(relay.at[rows(0, 1)]) + wide(part_ref.at[rows(right, 1)])
    ).astype(jnp.bfloat16)
    right_one.start()
    for half, needed in ((0, (right_zero, left_zero)), (1, (left_one, right_one))):
        needed[0].wait_recv()
        needed[1].wait_recv()
        total[rows(0, half), :] = (
            wide(part_ref.at[rows(me, half)])
            + wide(side.at[rows(0, half)])
            + wide(side.at[rows(1, half)])
        ).astype(jnp.bfloat16)
        back[half].start()
    back[0].wait_recv()
    back[1].wait_recv()
    table_out[...], state_out[...] = adagrad_block(
        table_ref[...], state_ref[...], wide(got), diagonal()
    )
    for sent in (first, second, left_one, right_zero, left_zero, right_one, *back):
        sent.wait_send()


def reduced(mask, collective_id, dst_part, table, state):
    vmem = pl.BlockSpec(memory_space=pltpu.VMEM)
    low = jnp.bfloat16
    return pl.pallas_call(
        functools.partial(reduce_kernel, mask),
        out_shape=(
            jax.ShapeDtypeStruct(table.shape, jnp.float32),
            jax.ShapeDtypeStruct(state.shape, jnp.float32),
        ),
        in_specs=[vmem] * 3,
        out_specs=(vmem, vmem),
        scratch_shapes=[
            pltpu.VMEM((TILE, D), low),
            pltpu.VMEM((TILE, D), low),
            pltpu.VMEM((2 * TILE, D), low),
            pltpu.VMEM((TILE, D), low),
            pltpu.VMEM((TILE, D), low),
            pltpu.SemaphoreType.DMA((8,)),
            pltpu.SemaphoreType.DMA((8,)),
        ],
        compiler_params=pltpu.CompilerParams(
            collective_id=collective_id, has_side_effects=True, vmem_limit_bytes=16 * 2**20
        ),
    )(dst_part, table, state)


def by_mask(make, first_id, round_mask, *args):
    last = lax.axis_size("bucket")
    branches = [functools.partial(make, mask, first_id + mask) for mask in range(1, last)]
    return lax.switch(round_mask - 1, branches, *args)


UNROLL = 4


def tile_kernel(code_ref, rel_id_ref, count_ref, src_ref, part_ref, rel_ref, state_ref,
    table_out, state_out, dst_out, src_low, src_grad, dst_grad
):
    src_low[...] = src_ref[...].astype(jnp.bfloat16).astype(jnp.float32)
    src_grad[...] = jnp.zeros_like(src_grad)
    dst_grad[...] = jnp.zeros_like(dst_grad)
    live = count_ref[0]
    row = lax.broadcasted_iota(jnp.int32, (TILE, TILE), 0)
    col = lax.broadcasted_iota(jnp.int32, (TILE, TILE), 1)
    shift = jnp.where(row == col, -0.5, 0.5).astype(jnp.float32)

    def step(group, carry):
        for lane in range(UNROLL):
            slot = group * UNROLL + lane
            code = code_ref[slot]
            s = pl.multiple_of((code // 4) * TILE, TILE)
            e = pl.multiple_of((code % 4) * TILE, TILE)
            rel = rel_ref[pl.ds(rel_id_ref[slot], 1), :]
            src_rel = (src_low[pl.ds(s, TILE), :] * rel).astype(jnp.bfloat16)
            dst = part_ref[pl.ds(e, TILE), :]
            scores = lax.dot_general(
                src_rel, dst, (((1,), (1,)), ((), ())), preferred_element_type=jnp.float32
            )
            on = jnp.where(slot < live, 1.0, 0.0).astype(jnp.float32)
            slope = ((jnp.tanh(scores * (0.5 * D**-0.5)) * 0.5 + shift) * on).astype(jnp.bfloat16)
            src_term = jnp.dot(slope, dst, preferred_element_type=jnp.float32)
            dst_term = lax.dot_general(
                slope, src_rel, (((0,), (0,)), ((), ())), preferred_element_type=jnp.float32
            )
            src_grad[pl.ds(s, TILE), :] += src_term * rel
            dst_grad[pl.ds(e, TILE), :] += dst_term
        return carry

    lax.fori_loop(0, (live + UNROLL - 1) // UNROLL, step, 0)
    diag = row == col
    for block in range(src_ref.shape[0] // TILE):
        at = slice(block * TILE, (block + 1) * TILE)
        table_out[at, :], state_out[block : block + 1, :] = adagrad_block(
            src_ref[at, :], state_ref[block : block + 1, :], src_grad[at, :] * D**-0.5, diag
        )
    dst_out[...] = (dst_grad[...] * D**-0.5).astype(jnp.bfloat16)


def tile_work(src_table, src_state, partition, tile_list, rel_list, live_count, rel_table):
    smem = pl.BlockSpec(memory_space=pltpu.SMEM)
    vmem = pl.BlockSpec(memory_space=pltpu.VMEM)
    return pl.pallas_call(
        tile_kernel,
        out_shape=(
            jax.ShapeDtypeStruct(src_table.shape, jnp.float32),
            jax.ShapeDtypeStruct(src_state.shape, jnp.float32),
            jax.ShapeDtypeStruct(partition.shape, jnp.bfloat16),
        ),
        in_specs=[smem, smem, smem, vmem, vmem, vmem, vmem],
        out_specs=(vmem, vmem, vmem),
        scratch_shapes=[
            pltpu.VMEM(src_table.shape, jnp.float32),
            pltpu.VMEM(src_table.shape, jnp.float32),
            pltpu.VMEM(partition.shape, jnp.float32),
        ],
        compiler_params=pltpu.CompilerParams(vmem_limit_bytes=32 * 2**20),
    )(tile_list, rel_list, live_count, src_table, partition, rel_table, src_state)


def per_device(
    src_table, src_state, dst_table, dst_state, rel_table, partners, tiles, tile_rel, counts
):
    src_state = src_state.reshape(-1, TILE)
    dst_state = dst_state.reshape(-1, TILE)
    for round_index in range(ROUNDS):
        round_mask = partners[round_index, 0]
        first_id = round_index * 2 * lax.axis_size("bucket")
        partition = by_mask(gathered, first_id, round_mask, dst_table)
        src_table, src_state, dst_part = tile_work(
            src_table,
            src_state,
            partition,
            tiles[0, 0, round_index],
            tile_rel[0, 0, round_index],
            counts[0, 0, round_index : round_index + 1],
            rel_table,
        )
        dst_table, dst_state = by_mask(
            reduced, first_id + lax.axis_size("bucket"), round_mask, dst_part, dst_table, dst_state
        )
    return (src_table, src_state.reshape(-1), dst_table, dst_state.reshape(-1))


def solution(mesh):
    in_specs = (
        P(("bucket", "rep"), None),
        P(("bucket", "rep")),
        P(("bucket", "rep"), None),
        P(("bucket", "rep")),
        P(),
        P(),
        P("bucket", "rep", None, None),
        P("bucket", "rep", None, None),
        P("bucket", "rep", None),
    )
    out_specs = (
        P(("bucket", "rep"), None),
        P(("bucket", "rep")),
        P(("bucket", "rep"), None),
        P(("bucket", "rep")),
    )
    return jax.shard_map(
        per_device, mesh=mesh, in_specs=in_specs, out_specs=out_specs, check_vma=False
    )
```

```python
import functools

import jax
import jax.numpy as jnp
from jax import lax
from jax.experimental import pallas as pl
from jax.experimental.pallas import tpu as pltpu
from jax.sharding import PartitionSpec as P

D = 256
TILE = 128
ROUNDS = 2


learn_rate = 0.1


HALF = TILE // 2
MESH = pl.DeviceIdType.MESH


def paired(mask):
    me = lax.axis_index("bucket")
    other = me
    for bit in range(mask.bit_length()):
        if mask >> bit & 1:
            other = other + (1 << bit) * (1 - 2 * lax.rem(lax.div(me, 1 << bit), 2))
    return other


def around():
    me = lax.axis_index("rep")
    return me, lax.rem(me + 3, 4), lax.rem(me + 1, 4), lax.rem(me + 2, 4)


def greet(devices):
    barrier = pltpu.get_barrier_semaphore()
    for device in devices:
        pl.semaphore_signal(barrier, inc=1, device_id=device, device_id_type=MESH)
    pl.semaphore_wait(barrier, len(devices))


def rows(quarter, half):
    return pl.ds(pl.multiple_of(quarter * TILE + half * HALF, HALF), HALF)


def gather_kernel(mask, low_ref, part_ref, send, recv):
    me, left, right, far = around()
    to_left, to_right, to_pair = {"rep": left}, {"rep": right}, {"bucket": paired(mask)}

    def copy(slot, src, dst, device):
        return pltpu.make_async_remote_copy(
            src, dst, send.at[slot], recv.at[slot], device_id=device, device_id_type=MESH
        )

    greet((to_pair, to_left, to_right) if mask else (to_left, to_right))
    own = [part_ref.at[rows(me, half)] for half in range(2)]
    if mask:
        hop = [copy(half, low_ref.at[rows(0, half)], own[half], to_pair) for half in range(2)]
        hop[0].start()
        hop[1].start()
    else:
        part_ref[pl.ds(pl.multiple_of(me * TILE, TILE), TILE), :] = low_ref[...]
        hop = []
    going_right = [copy(2 + half, own[half], own[half], to_right) for half in range(2)]
    going_left = [copy(4 + half, own[half], own[half], to_left) for half in range(2)]
    if mask:
        hop[0].wait_recv()
    going_right[0].start()
    going_left[0].start()
    if mask:
        hop[1].wait_recv()
    going_left[1].start()
    going_right[1].start()
    passed = part_ref.at[rows(left, 0)]
    on_right = copy(6, passed, passed, to_right)
    going_right[0].wait_recv()
    on_right.start()
    passed = part_ref.at[rows(right, 1)]
    on_left = copy(7, passed, passed, to_left)
    going_left[1].wait_recv()
    on_left.start()
    going_left[0].wait_recv()
    going_right[1].wait_recv()
    on_right.wait_recv()
    on_left.wait_recv()
    for sent in (*hop, *going_right, *going_left, on_right, on_left):
        sent.wait_send()


def gathered(mask, collective_id, low):
    vmem = pl.BlockSpec(memory_space=pltpu.VMEM)
    return pl.pallas_call(
        functools.partial(gather_kernel, mask),
        out_shape=jax.ShapeDtypeStruct((4 * TILE, D), jnp.bfloat16),
        in_specs=[vmem],
        out_specs=vmem,
        scratch_shapes=[pltpu.SemaphoreType.DMA((8,)), pltpu.SemaphoreType.DMA((8,))],
        compiler_params=pltpu.CompilerParams(
            collective_id=collective_id, has_side_effects=True, vmem_limit_bytes=16 * 2**20
        ),
    )(low)


def diagonal():
    row = lax.broadcasted_iota(jnp.int32, (TILE, TILE), 0)
    col = lax.broadcasted_iota(jnp.int32, (TILE, TILE), 1)
    return row == col


def adagrad_block(table, state_row, grad, diag):
    mean = jnp.sum(grad * grad, axis=1, keepdims=True) * (1 / D)
    state = jnp.sum(jnp.where(diag, state_row, 0.0), axis=1, keepdims=True) + mean
    table = table - grad * (learn_rate / jnp.sqrt(state))
    return table, jnp.sum(jnp.where(diag, state, 0.0), axis=0, keepdims=True)


def reduce_kernel(
    mask, part_ref, got, relay, added, side, total, send, recv
):
    me, left, right, far = around()
    to_left, to_right, to_pair = {"rep": left}, {"rep": right}, {"bucket": paired(mask)}

    def copy(slot, src, dst, device):
        return pltpu.make_async_remote_copy(
            src, dst, send.at[slot], recv.at[slot], device_id=device, device_id_type=MESH
        )

    def wide(ref):
        return ref[...].astype(jnp.float32)

    greet((to_pair, to_left, to_right) if mask else (to_left, to_right))
    first = copy(0, part_ref.at[rows(far, 0)], relay.at[rows(0, 0)], to_left)
    second = copy(1, part_ref.at[rows(far, 1)], relay.at[rows(0, 1)], to_right)
    left_one = copy(2, part_ref.at[rows(left, 1)], side.at[rows(1, 1)], to_left)
    right_zero = copy(3, part_ref.at[rows(right, 0)], side.at[rows(0, 0)], to_right)
    left_zero = copy(4, added.at[rows(0, 0)], side.at[rows(1, 0)], to_left)
    right_one = copy(5, added.at[rows(0, 1)], side.at[rows(0, 1)], to_right)
    if mask:
        back = [copy(6 + half, total.at[rows(0, half)], got.at[rows(0, half)], to_pair) for half in range(2)]
    else:
        back, total = [], got
    first.start()
    second.start()
    left_one.start()
    right_zero.start()
    first.wait_recv()
    added[rows(0, 0), :] = (
        wide(relay.at[rows(0, 0)]) + wide(part_ref.at[rows(left, 0)])
    ).astype(jnp.bfloat16)
    left_zero.start()
    second.wait_recv()
    added[rows(0, 1), :] = (
        wide(relay.at[rows(0, 1)]) + wide(part_ref.at[rows(right, 1)])
    ).astype(jnp.bfloat16)
    right_one.start()
    for half, needed in ((0, (right_zero, left_zero)), (1, (left_one, right_one))):
        needed[0].wait_recv()
        needed[1].wait_recv()
        total[rows(0, half), :] = (
            wide(part_ref.at[rows(me, half)])
            + wide(side.at[rows(0, half)])
            + wide(side.at[rows(1, half)])
        ).astype(jnp.bfloat16)
        if mask:
            back[half].start()
    for sent in back:
        sent.wait_recv()
    for sent in (first, second, left_one, right_zero, left_zero, right_one, *back):
        sent.wait_send()


def reduced(mask, collective_id, dst_part):
    vmem = pl.BlockSpec(memory_space=pltpu.VMEM)
    low = jnp.bfloat16
    return pl.pallas_call(
        functools.partial(reduce_kernel, mask),
        out_shape=jax.ShapeDtypeStruct((TILE, D), low),
        in_specs=[vmem],
        out_specs=vmem,
        scratch_shapes=[
            pltpu.VMEM((TILE, D), low),
            pltpu.VMEM((TILE, D), low),
            pltpu.VMEM((2 * TILE, D), low),
            pltpu.VMEM((TILE, D), low),
            pltpu.SemaphoreType.DMA((8,)),
            pltpu.SemaphoreType.DMA((8,)),
        ],
        compiler_params=pltpu.CompilerParams(
            collective_id=collective_id, has_side_effects=True, vmem_limit_bytes=16 * 2**20
        ),
    )(dst_part)


def permute_kernel(mask, rows_ref, moved_ref, send, recv):
    to_pair = {"bucket": paired(mask)}
    greet((to_pair,))
    copy = pltpu.make_async_remote_copy(
        rows_ref, moved_ref, send, recv, device_id=to_pair, device_id_type=MESH
    )
    copy.start()
    copy.wait()


def permuted(mask, collective_id, block):
    if not mask:
        return block
    vmem = pl.BlockSpec(memory_space=pltpu.VMEM)
    return pl.pallas_call(
        functools.partial(permute_kernel, mask),
        out_shape=jax.ShapeDtypeStruct(block.shape, block.dtype),
        in_specs=[vmem],
        out_specs=vmem,
        scratch_shapes=[pltpu.SemaphoreType.DMA, pltpu.SemaphoreType.DMA],
        compiler_params=pltpu.CompilerParams(
            collective_id=collective_id, has_side_effects=True, vmem_limit_bytes=16 * 2**20
        ),
    )(block)


def adagrad_kernel(table_ref, state_ref, grad_ref, table_out, state_out, low_out):
    table_out[...], state_out[...] = adagrad_block(
        table_ref[...], state_ref[...], grad_ref[...].astype(jnp.float32), diagonal()
    )
    low_out[...] = table_out[...].astype(jnp.bfloat16)


def updated(table, state, grad):
    vmem = pl.BlockSpec(memory_space=pltpu.VMEM)
    return pl.pallas_call(
        adagrad_kernel,
        out_shape=(
            jax.ShapeDtypeStruct(table.shape, jnp.float32),
            jax.ShapeDtypeStruct(state.shape, jnp.float32),
            jax.ShapeDtypeStruct(grad.shape, jnp.bfloat16),
        ),
        in_specs=[vmem] * 3,
        out_specs=(vmem,) * 3,
        compiler_params=pltpu.CompilerParams(vmem_limit_bytes=16 * 2**20),
    )(table, state, grad)


Y_MASKS = tuple(y << 2 for y in range(8))
OTHER_MASKS = tuple((x << 5) + low for x in range(4) for low in range(4))


def along_y(make, first_id, round_mask, block):
    branches = [functools.partial(make, mask, first_id + i) for i, mask in enumerate(Y_MASKS)]
    return lax.switch((round_mask >> 2) & 7, branches, block)


def along_others(first_id, round_mask, block):
    branches = [
        functools.partial(permuted, mask, first_id + i) for i, mask in enumerate(OTHER_MASKS)
    ]
    return lax.switch((round_mask >> 5) * 4 + (round_mask & 3), branches, block)


UNROLL = 4


def tile_kernel(round_index, code_ref, rel_id_ref, count_ref, src_ref, part_ref, rel_ref, state_ref,
    table_out, state_out, dst_out, src_low, src_grad, dst_grad
):
    src_low[...] = src_ref[...].astype(jnp.bfloat16).astype(jnp.float32)
    src_grad[...] = jnp.zeros_like(src_grad)
    dst_grad[...] = jnp.zeros_like(dst_grad)
    live = count_ref[0, 0, round_index]
    row = lax.broadcasted_iota(jnp.int32, (TILE, TILE), 0)
    col = lax.broadcasted_iota(jnp.int32, (TILE, TILE), 1)
    shift = jnp.where(row == col, -0.5, 0.5).astype(jnp.float32)

    def step(group, carry):
        for lane in range(UNROLL):
            slot = group * UNROLL + lane
            code = code_ref[0, 0, round_index, slot]
            s = pl.multiple_of((code // 4) * TILE, TILE)
            e = pl.multiple_of((code % 4) * TILE, TILE)
            rel = rel_ref[pl.ds(rel_id_ref[0, 0, round_index, slot], 1), :]
            src_rel = (src_low[pl.ds(s, TILE), :] * rel).astype(jnp.bfloat16)
            dst = part_ref[pl.ds(e, TILE), :]
            scores = lax.dot_general(
                src_rel, dst, (((1,), (1,)), ((), ())), preferred_element_type=jnp.float32
            )
            on = jnp.where(slot < live, 1.0, 0.0).astype(jnp.float32)
            slope = ((jnp.tanh(scores * (0.5 * D**-0.5)) * 0.5 + shift) * on).astype(jnp.bfloat16)
            src_term = jnp.dot(slope, dst, preferred_element_type=jnp.float32)
            dst_term = lax.dot_general(
                slope, src_rel, (((0,), (0,)), ((), ())), preferred_element_type=jnp.float32
            )
            src_grad[pl.ds(s, TILE), :] += src_term * rel
            dst_grad[pl.ds(e, TILE), :] += dst_term
        return carry

    lax.fori_loop(0, (live + UNROLL - 1) // UNROLL, step, 0)
    diag = row == col
    for block in range(src_ref.shape[0] // TILE):
        at = slice(block * TILE, (block + 1) * TILE)
        table_out[at, :], state_out[block : block + 1, :] = adagrad_block(
            src_ref[at, :], state_ref[block : block + 1, :], src_grad[at, :] * D**-0.5, diag
        )
    dst_out[...] = (dst_grad[...] * D**-0.5).astype(jnp.bfloat16)


def tile_work(
    round_index, src_table, src_state, partition, tile_list, rel_list, live_count, rel_table
):
    smem = pl.BlockSpec(memory_space=pltpu.SMEM)
    vmem = pl.BlockSpec(memory_space=pltpu.VMEM)
    return pl.pallas_call(
        functools.partial(tile_kernel, round_index),
        out_shape=(
            jax.ShapeDtypeStruct(src_table.shape, jnp.float32),
            jax.ShapeDtypeStruct(src_state.shape, jnp.float32),
            jax.ShapeDtypeStruct(partition.shape, jnp.bfloat16),
        ),
        in_specs=[smem, smem, smem, vmem, vmem, vmem, vmem],
        out_specs=(vmem, vmem, vmem),
        scratch_shapes=[
            pltpu.VMEM(src_table.shape, jnp.float32),
            pltpu.VMEM(src_table.shape, jnp.float32),
            pltpu.VMEM(partition.shape, jnp.float32),
        ],
        compiler_params=pltpu.CompilerParams(vmem_limit_bytes=32 * 2**20),
    )(tile_list, rel_list, live_count, src_table, partition, rel_table, src_state)


def per_device(
    src_table, src_state, dst_table, dst_state, rel_table, partners, tiles, tile_rel, counts
):
    src_state = src_state.reshape(-1, TILE)
    dst_state = dst_state.reshape(-1, TILE)
    low = dst_table.astype(jnp.bfloat16)
    for round_index in range(ROUNDS):
        round_mask = partners[round_index, 0]
        first_id = round_index * 48
        moved = along_others(first_id, round_mask, low)
        partition = along_y(gathered, first_id + 16, round_mask, moved)
        src_table, src_state, dst_part = tile_work(
            round_index, src_table, src_state, partition, tiles, tile_rel, counts, rel_table
        )
        summed = along_y(reduced, first_id + 24, round_mask, dst_part)
        grad = along_others(first_id + 32, round_mask, summed)
        dst_table, dst_state, low = updated(dst_table, dst_state, grad)
    return (src_table, src_state.reshape(-1), dst_table, dst_state.reshape(-1))


def solution(mesh):
    in_specs = (
        P(("bucket", "rep"), None),
        P(("bucket", "rep")),
        P(("bucket", "rep"), None),
        P(("bucket", "rep")),
        P(),
        P(),
        P("bucket", "rep", None, None),
        P("bucket", "rep", None, None),
        P("bucket", "rep", None),
    )
    out_specs = (
        P(("bucket", "rep"), None),
        P(("bucket", "rep")),
        P(("bucket", "rep"), None),
        P(("bucket", "rep")),
    )
    return jax.shard_map(
        per_device, mesh=mesh, in_specs=in_specs, out_specs=out_specs, check_vma=False
    )
```

```python
import functools

import jax
import jax.numpy as jnp
from jax import lax
from jax.experimental import pallas as pl
from jax.experimental.pallas import tpu as pltpu
from jax.sharding import PartitionSpec as P

D = 256
TILE = 128
ROUNDS = 2


learn_rate = 0.1


HALF = TILE // 2
MESH = pl.DeviceIdType.MESH


def paired(mask):
    me = lax.axis_index("bucket")
    other = me
    for bit in range(mask.bit_length()):
        if mask >> bit & 1:
            other = other + (1 << bit) * (1 - 2 * lax.rem(lax.div(me, 1 << bit), 2))
    return other


def around():
    me = lax.axis_index("rep")
    return me, lax.rem(me + 3, 4), lax.rem(me + 1, 4), lax.rem(me + 2, 4)


def greet(devices):
    barrier = pltpu.get_barrier_semaphore()
    for device in devices:
        pl.semaphore_signal(barrier, inc=1, device_id=device, device_id_type=MESH)
    pl.semaphore_wait(barrier, len(devices))


def rows(quarter, half):
    return pl.ds(pl.multiple_of(quarter * TILE + half * HALF, HALF), HALF)


def gather_kernel(mask, low_ref, part_ref, send, recv):
    me, left, right, far = around()
    to_left, to_right, to_pair = {"rep": left}, {"rep": right}, {"bucket": paired(mask)}

    def copy(slot, src, dst, device):
        return pltpu.make_async_remote_copy(
            src, dst, send.at[slot], recv.at[slot], device_id=device, device_id_type=MESH
        )

    greet((to_pair, to_left, to_right) if mask else (to_left, to_right))
    own = [part_ref.at[rows(me, half)] for half in range(2)]
    if mask:
        hop = [copy(half, low_ref.at[rows(0, half)], own[half], to_pair) for half in range(2)]
        hop[0].start()
        hop[1].start()
    else:
        part_ref[pl.ds(pl.multiple_of(me * TILE, TILE), TILE), :] = low_ref[...]
        hop = []
    going_right = [copy(2 + half, own[half], own[half], to_right) for half in range(2)]
    going_left = [copy(4 + half, own[half], own[half], to_left) for half in range(2)]
    if mask:
        hop[0].wait_recv()
    going_right[0].start()
    going_left[0].start()
    if mask:
        hop[1].wait_recv()
    going_left[1].start()
    going_right[1].start()
    passed = part_ref.at[rows(left, 0)]
    on_right = copy(6, passed, passed, to_right)
    going_right[0].wait_recv()
    on_right.start()
    passed = part_ref.at[rows(right, 1)]
    on_left = copy(7, passed, passed, to_left)
    going_left[1].wait_recv()
    on_left.start()
    going_left[0].wait_recv()
    going_right[1].wait_recv()
    on_right.wait_recv()
    on_left.wait_recv()
    for sent in (*hop, *going_right, *going_left, on_right, on_left):
        sent.wait_send()


def gathered(mask, collective_id, low):
    vmem = pl.BlockSpec(memory_space=pltpu.VMEM)
    return pl.pallas_call(
        functools.partial(gather_kernel, mask),
        out_shape=jax.ShapeDtypeStruct((4 * TILE, D), jnp.bfloat16),
        in_specs=[vmem],
        out_specs=vmem,
        scratch_shapes=[pltpu.SemaphoreType.DMA((8,)), pltpu.SemaphoreType.DMA((8,))],
        compiler_params=pltpu.CompilerParams(
            collective_id=collective_id, has_side_effects=True, vmem_limit_bytes=16 * 2**20
        ),
    )(low)


def diagonal():
    row = lax.broadcasted_iota(jnp.int32, (TILE, TILE), 0)
    col = lax.broadcasted_iota(jnp.int32, (TILE, TILE), 1)
    return row == col


def adagrad_block(table, state_row, grad, diag):
    mean = jnp.sum(grad * grad, axis=1, keepdims=True) * (1 / D)
    state = jnp.sum(jnp.where(diag, state_row, 0.0), axis=1, keepdims=True) + mean
    table = table - grad * (learn_rate / jnp.sqrt(state))
    return table, jnp.sum(jnp.where(diag, state, 0.0), axis=0, keepdims=True)


def reduce_kernel(
    mask, part_ref, got, relay, added, side, total, send, recv
):
    me, left, right, far = around()
    to_left, to_right, to_pair = {"rep": left}, {"rep": right}, {"bucket": paired(mask)}

    def copy(slot, src, dst, device):
        return pltpu.make_async_remote_copy(
            src, dst, send.at[slot], recv.at[slot], device_id=device, device_id_type=MESH
        )

    def wide(ref):
        return ref[...].astype(jnp.float32)

    greet((to_pair, to_left, to_right) if mask else (to_left, to_right))
    first = copy(0, part_ref.at[rows(far, 0)], relay.at[rows(0, 0)], to_left)
    second = copy(1, part_ref.at[rows(far, 1)], relay.at[rows(0, 1)], to_right)
    left_one = copy(2, part_ref.at[rows(left, 1)], side.at[rows(1, 1)], to_left)
    right_zero = copy(3, part_ref.at[rows(right, 0)], side.at[rows(0, 0)], to_right)
    left_zero = copy(4, added.at[rows(0, 0)], side.at[rows(1, 0)], to_left)
    right_one = copy(5, added.at[rows(0, 1)], side.at[rows(0, 1)], to_right)
    if mask:
        back = [copy(6 + half, total.at[rows(0, half)], got.at[rows(0, half)], to_pair) for half in range(2)]
    else:
        back, total = [], got
    first.start()
    second.start()
    left_one.start()
    right_zero.start()
    first.wait_recv()
    added[rows(0, 0), :] = (
        wide(relay.at[rows(0, 0)]) + wide(part_ref.at[rows(left, 0)])
    ).astype(jnp.bfloat16)
    left_zero.start()
    second.wait_recv()
    added[rows(0, 1), :] = (
        wide(relay.at[rows(0, 1)]) + wide(part_ref.at[rows(right, 1)])
    ).astype(jnp.bfloat16)
    right_one.start()
    for half, needed in ((0, (right_zero, left_zero)), (1, (left_one, right_one))):
        needed[0].wait_recv()
        needed[1].wait_recv()
        total[rows(0, half), :] = (
            wide(part_ref.at[rows(me, half)])
            + wide(side.at[rows(0, half)])
            + wide(side.at[rows(1, half)])
        ).astype(jnp.bfloat16)
        if mask:
            back[half].start()
    for sent in back:
        sent.wait_recv()
    for sent in (first, second, left_one, right_zero, left_zero, right_one, *back):
        sent.wait_send()


def reduced(mask, collective_id, dst_part):
    vmem = pl.BlockSpec(memory_space=pltpu.VMEM)
    low = jnp.bfloat16
    return pl.pallas_call(
        functools.partial(reduce_kernel, mask),
        out_shape=jax.ShapeDtypeStruct((TILE, D), low),
        in_specs=[vmem],
        out_specs=vmem,
        scratch_shapes=[
            pltpu.VMEM((TILE, D), low),
            pltpu.VMEM((TILE, D), low),
            pltpu.VMEM((2 * TILE, D), low),
            pltpu.VMEM((TILE, D), low),
            pltpu.SemaphoreType.DMA((8,)),
            pltpu.SemaphoreType.DMA((8,)),
        ],
        compiler_params=pltpu.CompilerParams(
            collective_id=collective_id, has_side_effects=True, vmem_limit_bytes=16 * 2**20
        ),
    )(dst_part)


def permute_kernel(mask, rows_ref, moved_ref, send, recv):
    to_pair = {"bucket": paired(mask)}
    greet((to_pair,))
    copy = pltpu.make_async_remote_copy(
        rows_ref, moved_ref, send, recv, device_id=to_pair, device_id_type=MESH
    )
    copy.start()
    copy.wait()


def permuted(mask, collective_id, block):
    if not mask:
        return block
    vmem = pl.BlockSpec(memory_space=pltpu.VMEM)
    return pl.pallas_call(
        functools.partial(permute_kernel, mask),
        out_shape=jax.ShapeDtypeStruct(block.shape, block.dtype),
        in_specs=[vmem],
        out_specs=vmem,
        scratch_shapes=[pltpu.SemaphoreType.DMA, pltpu.SemaphoreType.DMA],
        compiler_params=pltpu.CompilerParams(
            collective_id=collective_id, has_side_effects=True, vmem_limit_bytes=16 * 2**20
        ),
    )(block)


def adagrad_kernel(table_ref, state_ref, grad_ref, table_out, state_out, low_out):
    table_out[...], state_out[...] = adagrad_block(
        table_ref[...], state_ref[...], grad_ref[...].astype(jnp.float32), diagonal()
    )
    low_out[...] = table_out[...].astype(jnp.bfloat16)


def updated(table, state, grad):
    vmem = pl.BlockSpec(memory_space=pltpu.VMEM)
    return pl.pallas_call(
        adagrad_kernel,
        out_shape=(
            jax.ShapeDtypeStruct(table.shape, jnp.float32),
            jax.ShapeDtypeStruct(state.shape, jnp.float32),
            jax.ShapeDtypeStruct(grad.shape, jnp.bfloat16),
        ),
        in_specs=[vmem] * 3,
        out_specs=(vmem,) * 3,
        compiler_params=pltpu.CompilerParams(vmem_limit_bytes=16 * 2**20),
    )(table, state, grad)


Y_MASKS = tuple(y << 2 for y in range(8))
OTHER_MASKS = tuple((x << 5) + low for x in range(4) for low in range(4))


def along_y(make, first_id, round_mask, block):
    branches = [functools.partial(make, mask, first_id + i) for i, mask in enumerate(Y_MASKS)]
    return lax.switch((round_mask >> 2) & 7, branches, block)


def along_others(round_mask, block):
    branches = [
        functools.partial(permuted, mask, i) for i, mask in enumerate(OTHER_MASKS)
    ]
    return lax.switch((round_mask >> 5) * 4 + (round_mask & 3), branches, block)


UNROLL = 4


def tile_kernel(round_index, code_ref, rel_id_ref, count_ref, src_ref, part_ref, rel_ref, state_ref,
    table_out, state_out, dst_out, src_low, src_grad, dst_grad
):
    src_low[...] = src_ref[...].astype(jnp.bfloat16).astype(jnp.float32)
    src_grad[...] = jnp.zeros_like(src_grad)
    dst_grad[...] = jnp.zeros_like(dst_grad)
    live = count_ref[0, 0, round_index]
    row = lax.broadcasted_iota(jnp.int32, (TILE, TILE), 0)
    col = lax.broadcasted_iota(jnp.int32, (TILE, TILE), 1)
    shift = jnp.where(row == col, -0.5, 0.5).astype(jnp.float32)

    def step(group, carry):
        for lane in range(UNROLL):
            slot = group * UNROLL + lane
            code = code_ref[0, 0, round_index, slot]
            s = pl.multiple_of((code // 4) * TILE, TILE)
            e = pl.multiple_of((code % 4) * TILE, TILE)
            rel = rel_ref[pl.ds(rel_id_ref[0, 0, round_index, slot], 1), :]
            src_rel = (src_low[pl.ds(s, TILE), :] * rel).astype(jnp.bfloat16)
            dst = part_ref[pl.ds(e, TILE), :]
            scores = lax.dot_general(
                src_rel, dst, (((1,), (1,)), ((), ())), preferred_element_type=jnp.float32
            )
            on = jnp.where(slot < live, 1.0, 0.0).astype(jnp.float32)
            slope = ((jnp.tanh(scores * (0.5 * D**-0.5)) * 0.5 + shift) * on).astype(jnp.bfloat16)
            src_term = jnp.dot(slope, dst, preferred_element_type=jnp.float32)
            dst_term = lax.dot_general(
                slope, src_rel, (((0,), (0,)), ((), ())), preferred_element_type=jnp.float32
            )
            src_grad[pl.ds(s, TILE), :] += src_term * rel
            dst_grad[pl.ds(e, TILE), :] += dst_term
        return carry

    lax.fori_loop(0, (live + UNROLL - 1) // UNROLL, step, 0)
    diag = row == col
    for block in range(src_ref.shape[0] // TILE):
        at = slice(block * TILE, (block + 1) * TILE)
        table_out[at, :], state_out[block : block + 1, :] = adagrad_block(
            src_ref[at, :], state_ref[block : block + 1, :], src_grad[at, :] * D**-0.5, diag
        )
    dst_out[...] = (dst_grad[...] * D**-0.5).astype(jnp.bfloat16)


def tile_work(
    round_index, src_table, src_state, partition, tile_list, rel_list, live_count, rel_table
):
    smem = pl.BlockSpec(memory_space=pltpu.SMEM)
    vmem = pl.BlockSpec(memory_space=pltpu.VMEM)
    return pl.pallas_call(
        functools.partial(tile_kernel, round_index),
        out_shape=(
            jax.ShapeDtypeStruct(src_table.shape, jnp.float32),
            jax.ShapeDtypeStruct(src_state.shape, jnp.float32),
            jax.ShapeDtypeStruct(partition.shape, jnp.bfloat16),
        ),
        in_specs=[smem, smem, smem, vmem, vmem, vmem, vmem],
        out_specs=(vmem, vmem, vmem),
        scratch_shapes=[
            pltpu.VMEM(src_table.shape, jnp.float32),
            pltpu.VMEM(src_table.shape, jnp.float32),
            pltpu.VMEM(partition.shape, jnp.float32),
        ],
        compiler_params=pltpu.CompilerParams(vmem_limit_bytes=32 * 2**20),
    )(tile_list, rel_list, live_count, src_table, partition, rel_table, src_state)


def per_device(
    src_table, src_state, dst_table, dst_state, rel_table, partners, tiles, tile_rel, counts
):
    src_state = src_state.reshape(-1, TILE)
    dst_state = dst_state.reshape(-1, TILE)
    low = dst_table.astype(jnp.bfloat16)
    for round_index in range(ROUNDS):
        round_mask = partners[round_index, 0]
        moved = along_others(round_mask, low)
        partition = along_y(gathered, 16, round_mask, moved)
        src_table, src_state, dst_part = tile_work(
            round_index, src_table, src_state, partition, tiles, tile_rel, counts, rel_table
        )
        summed = along_y(reduced, 24, round_mask, dst_part)
        grad = along_others(round_mask, summed)
        dst_table, dst_state, low = updated(dst_table, dst_state, grad)
    return (src_table, src_state.reshape(-1), dst_table, dst_state.reshape(-1))


def solution(mesh):
    in_specs = (
        P(("bucket", "rep"), None),
        P(("bucket", "rep")),
        P(("bucket", "rep"), None),
        P(("bucket", "rep")),
        P(),
        P(),
        P("bucket", "rep", None, None),
        P("bucket", "rep", None, None),
        P("bucket", "rep", None),
    )
    out_specs = (
        P(("bucket", "rep"), None),
        P(("bucket", "rep")),
        P(("bucket", "rep"), None),
        P(("bucket", "rep")),
    )
    return jax.shard_map(
        per_device, mesh=mesh, in_specs=in_specs, out_specs=out_specs, check_vma=False
    )
```

```python
import functools

import jax
import jax.numpy as jnp
from jax import lax
from jax.experimental import pallas as pl
from jax.experimental.pallas import tpu as pltpu
from jax.sharding import PartitionSpec as P

D = 256
TILE = 128
ROUNDS = 2


learn_rate = 0.1


CHUNK = TILE // 4
ORDER = (0, 2, 1, 3)
MESH = pl.DeviceIdType.MESH


def paired(mask):
    me = lax.axis_index("bucket")
    other = me
    for bit in range(mask.bit_length()):
        if mask >> bit & 1:
            other = other + (1 << bit) * (1 - 2 * lax.rem(lax.div(me, 1 << bit), 2))
    return other


def around():
    me = lax.axis_index("rep")
    return me, lax.rem(me + 3, 4), lax.rem(me + 1, 4), lax.rem(me + 2, 4)


def greet(devices):
    barrier = pltpu.get_barrier_semaphore()
    for device in devices:
        pl.semaphore_signal(barrier, inc=1, device_id=device, device_id_type=MESH)
    pl.semaphore_wait(barrier, len(devices))


def rows(quarter, chunk):
    return pl.ds(pl.multiple_of(quarter * TILE + chunk * CHUNK, CHUNK), CHUNK)


def gather_kernel(mask, low_ref, part_ref, send, recv):
    me, left, right, far = around()
    to_left, to_right, to_pair = {"rep": left}, {"rep": right}, {"bucket": paired(mask)}

    def copy(slot, src, dst, device):
        return pltpu.make_async_remote_copy(
            src, dst, send.at[slot], recv.at[slot], device_id=device, device_id_type=MESH
        )

    greet((to_pair, to_left, to_right) if mask else (to_left, to_right))
    own = [part_ref.at[rows(me, chunk)] for chunk in range(4)]
    hop = {}
    if mask:
        for chunk in ORDER:
            hop[chunk] = copy(chunk, low_ref.at[rows(0, chunk)], own[chunk], to_pair)
            hop[chunk].start()
    else:
        part_ref[pl.ds(pl.multiple_of(me * TILE, TILE), TILE), :] = low_ref[...]
    going_right = [copy(4 + chunk, own[chunk], own[chunk], to_right) for chunk in range(4)]
    going_left = [copy(8 + chunk, own[chunk], own[chunk], to_left) for chunk in range(4)]
    for chunk in ORDER:
        if mask:
            hop[chunk].wait_recv()
        near = (going_right, going_left) if chunk < 2 else (going_left, going_right)
        near[0][chunk].start()
        near[1][chunk].start()
    onward = []
    for chunk in ORDER:
        came, source, device = (
            (going_right, left, to_right) if chunk < 2 else (going_left, right, to_left)
        )
        came[chunk].wait_recv()
        passed = part_ref.at[rows(source, chunk)]
        onward.append(copy(12 + chunk, passed, passed, device))
        onward[-1].start()
    for chunk in range(4):
        (going_left if chunk < 2 else going_right)[chunk].wait_recv()
    for passed in onward:
        passed.wait_recv()
    for sent in (*hop.values(), *going_right, *going_left, *onward):
        sent.wait_send()


def gathered(mask, collective_id, low):
    vmem = pl.BlockSpec(memory_space=pltpu.VMEM)
    return pl.pallas_call(
        functools.partial(gather_kernel, mask),
        out_shape=jax.ShapeDtypeStruct((4 * TILE, D), jnp.bfloat16),
        in_specs=[vmem],
        out_specs=vmem,
        scratch_shapes=[pltpu.SemaphoreType.DMA((16,)), pltpu.SemaphoreType.DMA((16,))],
        compiler_params=pltpu.CompilerParams(
            collective_id=collective_id, has_side_effects=True, vmem_limit_bytes=16 * 2**20
        ),
    )(low)


def diagonal():
    row = lax.broadcasted_iota(jnp.int32, (TILE, TILE), 0)
    col = lax.broadcasted_iota(jnp.int32, (TILE, TILE), 1)
    return row == col


def adagrad_block(table, state_row, grad, diag):
    mean = jnp.sum(grad * grad, axis=1, keepdims=True) * (1 / D)
    state = jnp.sum(jnp.where(diag, state_row, 0.0), axis=1, keepdims=True) + mean
    table = table - grad * (learn_rate / jnp.sqrt(state))
    return table, jnp.sum(jnp.where(diag, state, 0.0), axis=0, keepdims=True)


def reduce_kernel(
    mask, part_ref, got, relay, added, side, total, send, recv
):
    me, left, right, far = around()
    to_left, to_right, to_pair = {"rep": left}, {"rep": right}, {"bucket": paired(mask)}

    def copy(slot, src, dst, device):
        return pltpu.make_async_remote_copy(
            src, dst, send.at[slot], recv.at[slot], device_id=device, device_id_type=MESH
        )

    def wide(ref):
        return ref[...].astype(jnp.float32)

    greet((to_pair, to_left, to_right) if mask else (to_left, to_right))
    far_ones, near_ones, added_ones, back = {}, {}, {}, {}
    for chunk in ORDER:
        device = to_left if chunk < 2 else to_right
        far_ones[chunk] = copy(chunk, part_ref.at[rows(far, chunk)], relay.at[rows(0, chunk)], device)
        far_ones[chunk].start()
    for chunk in ORDER:
        owner, place, device = (right, 0, to_right) if chunk < 2 else (left, 1, to_left)
        near_ones[chunk] = copy(
            4 + chunk, part_ref.at[rows(owner, chunk)], side.at[rows(place, chunk)], device
        )
        near_ones[chunk].start()
    for chunk in ORDER:
        owner, place, device = (left, 1, to_left) if chunk < 2 else (right, 0, to_right)
        far_ones[chunk].wait_recv()
        added[rows(0, chunk), :] = (
            wide(relay.at[rows(0, chunk)]) + wide(part_ref.at[rows(owner, chunk)])
        ).astype(jnp.bfloat16)
        added_ones[chunk] = copy(
            8 + chunk, added.at[rows(0, chunk)], side.at[rows(place, chunk)], device
        )
        added_ones[chunk].start()
    for chunk in ORDER:
        near_ones[chunk].wait_recv()
        added_ones[chunk].wait_recv()
        (total if mask else got)[rows(0, chunk), :] = (
            wide(part_ref.at[rows(me, chunk)])
            + wide(side.at[rows(0, chunk)])
            + wide(side.at[rows(1, chunk)])
        ).astype(jnp.bfloat16)
        if mask:
            back[chunk] = copy(12 + chunk, total.at[rows(0, chunk)], got.at[rows(0, chunk)], to_pair)
            back[chunk].start()
    for sent in back.values():
        sent.wait_recv()
    for group in (far_ones, near_ones, added_ones, back):
        for sent in group.values():
            sent.wait_send()


def reduced(mask, collective_id, dst_part):
    vmem = pl.BlockSpec(memory_space=pltpu.VMEM)
    low = jnp.bfloat16
    return pl.pallas_call(
        functools.partial(reduce_kernel, mask),
        out_shape=jax.ShapeDtypeStruct((TILE, D), low),
        in_specs=[vmem],
        out_specs=vmem,
        scratch_shapes=[
            pltpu.VMEM((TILE, D), low),
            pltpu.VMEM((TILE, D), low),
            pltpu.VMEM((2 * TILE, D), low),
            pltpu.VMEM((TILE, D), low),
            pltpu.SemaphoreType.DMA((16,)),
            pltpu.SemaphoreType.DMA((16,)),
        ],
        compiler_params=pltpu.CompilerParams(
            collective_id=collective_id, has_side_effects=True, vmem_limit_bytes=16 * 2**20
        ),
    )(dst_part)


def permute_kernel(mask, rows_ref, moved_ref, send, recv):
    to_pair = {"bucket": paired(mask)}
    greet((to_pair,))
    copy = pltpu.make_async_remote_copy(
        rows_ref, moved_ref, send, recv, device_id=to_pair, device_id_type=MESH
    )
    copy.start()
    copy.wait()


def permuted(mask, collective_id, block):
    if not mask:
        return block
    vmem = pl.BlockSpec(memory_space=pltpu.VMEM)
    return pl.pallas_call(
        functools.partial(permute_kernel, mask),
        out_shape=jax.ShapeDtypeStruct(block.shape, block.dtype),
        in_specs=[vmem],
        out_specs=vmem,
        scratch_shapes=[pltpu.SemaphoreType.DMA, pltpu.SemaphoreType.DMA],
        compiler_params=pltpu.CompilerParams(
            collective_id=collective_id, has_side_effects=True, vmem_limit_bytes=16 * 2**20
        ),
    )(block)


def adagrad_kernel(table_ref, state_ref, grad_ref, table_out, state_out, low_out):
    table_out[...], state_out[...] = adagrad_block(
        table_ref[...], state_ref[...], grad_ref[...].astype(jnp.float32), diagonal()
    )
    low_out[...] = table_out[...].astype(jnp.bfloat16)


def updated(table, state, grad):
    vmem = pl.BlockSpec(memory_space=pltpu.VMEM)
    return pl.pallas_call(
        adagrad_kernel,
        out_shape=(
            jax.ShapeDtypeStruct(table.shape, jnp.float32),
            jax.ShapeDtypeStruct(state.shape, jnp.float32),
            jax.ShapeDtypeStruct(grad.shape, jnp.bfloat16),
        ),
        in_specs=[vmem] * 3,
        out_specs=(vmem,) * 3,
        compiler_params=pltpu.CompilerParams(vmem_limit_bytes=16 * 2**20),
    )(table, state, grad)


Y_MASKS = tuple(y << 2 for y in range(8))
OTHER_MASKS = tuple((x << 5) + low for x in range(4) for low in range(4))


def along_y(make, first_id, index, block):
    branches = [functools.partial(make, mask, first_id + i) for i, mask in enumerate(Y_MASKS)]
    return lax.switch(index, branches, block)


def along_others(index, block):
    branches = [functools.partial(permuted, mask, i) for i, mask in enumerate(OTHER_MASKS)]
    return lax.switch(index, branches, block)


def prepare_kernel(partners_ref, table_ref, low_ref, *index_refs):
    low_ref[...] = table_ref[...].astype(jnp.bfloat16)
    for round_index in range(ROUNDS):
        mask = partners_ref[round_index, 0]
        index_refs[2 * round_index][0, 0] = (mask >> 5) * 4 + (mask & 3)
        index_refs[2 * round_index + 1][0, 0] = (mask >> 2) & 7


def prepared(partners, table):
    smem = pl.BlockSpec(memory_space=pltpu.SMEM)
    vmem = pl.BlockSpec(memory_space=pltpu.VMEM)
    low, *indices = pl.pallas_call(
        prepare_kernel,
        out_shape=(
            jax.ShapeDtypeStruct(table.shape, jnp.bfloat16),
            *[jax.ShapeDtypeStruct((1, 1), jnp.int32)] * (2 * ROUNDS),
        ),
        in_specs=[smem, vmem],
        out_specs=(vmem, *[smem] * (2 * ROUNDS)),
        compiler_params=pltpu.CompilerParams(vmem_limit_bytes=16 * 2**20),
    )(partners, table)
    return low, [index[0, 0] for index in indices]


UNROLL = 16


def tile_kernel(round_index, code_ref, rel_id_ref, count_ref, src_ref, part_ref, rel_ref, state_ref,
    table_out, state_out, dst_out, src_low, src_grad, dst_grad
):
    src_low[...] = src_ref[...].astype(jnp.bfloat16).astype(jnp.float32)
    src_grad[...] = jnp.zeros_like(src_grad)
    dst_grad[...] = jnp.zeros_like(dst_grad)
    live = count_ref[0, 0, round_index]
    row = lax.broadcasted_iota(jnp.int32, (TILE, TILE), 0)
    col = lax.broadcasted_iota(jnp.int32, (TILE, TILE), 1)
    shift = jnp.where(row == col, -0.5, 0.5).astype(jnp.float32)

    def step(group, carry):
        lanes = range(UNROLL)
        slots = [group * UNROLL + lane for lane in lanes]
        codes = [code_ref[0, 0, round_index, slot] for slot in slots]
        src_at = [pl.ds(pl.multiple_of((code // 4) * TILE, TILE), TILE) for code in codes]
        dst_at = [pl.ds(pl.multiple_of((code % 4) * TILE, TILE), TILE) for code in codes]
        rels = [rel_ref[pl.ds(rel_id_ref[0, 0, round_index, slot], 1), :] for slot in slots]
        dsts = [part_ref[at, :] for at in dst_at]
        src_rels = [(src_low[src_at[lane], :] * rels[lane]).astype(jnp.bfloat16) for lane in lanes]
        scores = [
            lax.dot_general(
                src_rels[lane], dsts[lane], (((1,), (1,)), ((), ())), preferred_element_type=jnp.float32
            )
            for lane in lanes
        ]
        ons = [jnp.where(slot < live, 1.0, 0.0).astype(jnp.float32) for slot in slots]
        slopes = [
            ((jnp.tanh(scores[lane] * (0.5 * D**-0.5)) * 0.5 + shift) * ons[lane]).astype(jnp.bfloat16)
            for lane in lanes
        ]
        src_terms = [
            jnp.dot(slopes[lane], dsts[lane], preferred_element_type=jnp.float32) for lane in lanes
        ]
        dst_terms = [
            lax.dot_general(
                slopes[lane], src_rels[lane], (((0,), (0,)), ((), ())), preferred_element_type=jnp.float32
            )
            for lane in lanes
        ]
        for lane in lanes:
            src_grad[src_at[lane], :] += src_terms[lane] * rels[lane]
            dst_grad[dst_at[lane], :] += dst_terms[lane]
        return carry

    lax.fori_loop(0, (live + UNROLL - 1) // UNROLL, step, 0)
    diag = row == col
    for block in range(src_ref.shape[0] // TILE):
        at = slice(block * TILE, (block + 1) * TILE)
        table_out[at, :], state_out[block : block + 1, :] = adagrad_block(
            src_ref[at, :], state_ref[block : block + 1, :], src_grad[at, :] * D**-0.5, diag
        )
    dst_out[...] = (dst_grad[...] * D**-0.5).astype(jnp.bfloat16)


def tile_work(
    round_index, src_table, src_state, partition, tile_list, rel_list, live_count, rel_table
):
    smem = pl.BlockSpec(memory_space=pltpu.SMEM)
    vmem = pl.BlockSpec(memory_space=pltpu.VMEM)
    return pl.pallas_call(
        functools.partial(tile_kernel, round_index),
        out_shape=(
            jax.ShapeDtypeStruct(src_table.shape, jnp.float32),
            jax.ShapeDtypeStruct(src_state.shape, jnp.float32),
            jax.ShapeDtypeStruct(partition.shape, jnp.bfloat16),
        ),
        in_specs=[smem, smem, smem, vmem, vmem, vmem, vmem],
        out_specs=(vmem, vmem, vmem),
        scratch_shapes=[
            pltpu.VMEM(src_table.shape, jnp.float32),
            pltpu.VMEM(src_table.shape, jnp.float32),
            pltpu.VMEM(partition.shape, jnp.float32),
        ],
        compiler_params=pltpu.CompilerParams(vmem_limit_bytes=32 * 2**20),
    )(tile_list, rel_list, live_count, src_table, partition, rel_table, src_state)


def per_device(
    src_table, src_state, dst_table, dst_state, rel_table, partners, tiles, tile_rel, counts
):
    src_state = src_state.reshape(-1, TILE)
    dst_state = dst_state.reshape(-1, TILE)
    low, indices = prepared(partners, dst_table)
    for round_index in range(ROUNDS):
        others, y = indices[2 * round_index : 2 * round_index + 2]
        moved = along_others(others, low)
        partition = along_y(gathered, 16, y, moved)
        src_table, src_state, dst_part = tile_work(
            round_index, src_table, src_state, partition, tiles, tile_rel, counts, rel_table
        )
        summed = along_y(reduced, 24, y, dst_part)
        grad = along_others(others, summed)
        dst_table, dst_state, low = updated(dst_table, dst_state, grad)
    return (src_table, src_state.reshape(-1), dst_table, dst_state.reshape(-1))


def solution(mesh):
    in_specs = (
        P(("bucket", "rep"), None),
        P(("bucket", "rep")),
        P(("bucket", "rep"), None),
        P(("bucket", "rep")),
        P(),
        P(),
        P("bucket", "rep", None, None),
        P("bucket", "rep", None, None),
        P("bucket", "rep", None),
    )
    out_specs = (
        P(("bucket", "rep"), None),
        P(("bucket", "rep")),
        P(("bucket", "rep"), None),
        P(("bucket", "rep")),
    )
    return jax.shard_map(
        per_device, mesh=mesh, in_specs=in_specs, out_specs=out_specs, check_vma=False
    )
```

```python
import functools

import jax
import jax.numpy as jnp
from jax import lax
from jax.experimental import pallas as pl
from jax.experimental.pallas import tpu as pltpu
from jax.sharding import PartitionSpec as P

D = 256
TILE = 128
ROUNDS = 2


learn_rate = 0.1


CHUNK = TILE // 4
ORDER = (0, 2, 1, 3)
MESH = pl.DeviceIdType.MESH


def paired(mask):
    me = lax.axis_index("bucket")
    other = me
    for bit in range(mask.bit_length()):
        if mask >> bit & 1:
            other = other + (1 << bit) * (1 - 2 * lax.rem(lax.div(me, 1 << bit), 2))
    return other


def around():
    me = lax.axis_index("rep")
    return me, lax.rem(me + 3, 4), lax.rem(me + 1, 4), lax.rem(me + 2, 4)


def greet(devices):
    barrier = pltpu.get_barrier_semaphore()
    for device in devices:
        pl.semaphore_signal(barrier, inc=1, device_id=device, device_id_type=MESH)
    pl.semaphore_wait(barrier, len(devices))


def rows(quarter, chunk):
    return pl.ds(pl.multiple_of(quarter * TILE + chunk * CHUNK, CHUNK), CHUNK)


def gather_kernel(mask, low_ref, part_ref, send, recv):
    me, left, right, far = around()
    to_left, to_right, to_pair = {"rep": left}, {"rep": right}, {"bucket": paired(mask)}

    def copy(slot, src, dst, device):
        return pltpu.make_async_remote_copy(
            src, dst, send.at[slot], recv.at[slot], device_id=device, device_id_type=MESH
        )

    greet((to_pair, to_left, to_right) if mask else (to_left, to_right))
    own = [part_ref.at[rows(me, chunk)] for chunk in range(4)]
    hop = {}
    if mask:
        for chunk in ORDER:
            hop[chunk] = copy(chunk, low_ref.at[rows(0, chunk)], own[chunk], to_pair)
            hop[chunk].start()
    else:
        part_ref[pl.ds(pl.multiple_of(me * TILE, TILE), TILE), :] = low_ref[...]
    going_right = [copy(4 + chunk, own[chunk], own[chunk], to_right) for chunk in range(4)]
    going_left = [copy(8 + chunk, own[chunk], own[chunk], to_left) for chunk in range(4)]
    for chunk in ORDER:
        if mask:
            hop[chunk].wait_recv()
        near = (going_right, going_left) if chunk < 2 else (going_left, going_right)
        near[0][chunk].start()
        near[1][chunk].start()
    onward = []
    for chunk in ORDER:
        came, source, device = (
            (going_right, left, to_right) if chunk < 2 else (going_left, right, to_left)
        )
        came[chunk].wait_recv()
        passed = part_ref.at[rows(source, chunk)]
        onward.append(copy(12 + chunk, passed, passed, device))
        onward[-1].start()
    for sent in (*hop.values(), *going_right, *going_left):
        sent.wait_send()
    for chunk in range(4):
        (going_left if chunk < 2 else going_right)[chunk].wait_recv()
    for sent in onward:
        sent.wait_send()
    for passed in onward:
        passed.wait_recv()


def gathered(mask, collective_id, low):
    vmem = pl.BlockSpec(memory_space=pltpu.VMEM)
    return pl.pallas_call(
        functools.partial(gather_kernel, mask),
        out_shape=jax.ShapeDtypeStruct((4 * TILE, D), jnp.bfloat16),
        in_specs=[vmem],
        out_specs=vmem,
        scratch_shapes=[pltpu.SemaphoreType.DMA((16,)), pltpu.SemaphoreType.DMA((16,))],
        compiler_params=pltpu.CompilerParams(
            collective_id=collective_id, has_side_effects=True, vmem_limit_bytes=16 * 2**20
        ),
    )(low)


def diagonal():
    row = lax.broadcasted_iota(jnp.int32, (TILE, TILE), 0)
    col = lax.broadcasted_iota(jnp.int32, (TILE, TILE), 1)
    return row == col


def adagrad_block(table, state_row, grad, diag):
    mean = jnp.sum(grad * grad, axis=1, keepdims=True) * (1 / D)
    state = jnp.sum(jnp.where(diag, state_row, 0.0), axis=1, keepdims=True) + mean
    table = table - grad * (learn_rate / jnp.sqrt(state))
    return table, jnp.sum(jnp.where(diag, state, 0.0), axis=0, keepdims=True)


def reduce_kernel(
    mask, part_ref, got, relay, added, side, total, send, recv
):
    me, left, right, far = around()
    to_left, to_right, to_pair = {"rep": left}, {"rep": right}, {"bucket": paired(mask)}

    def copy(slot, src, dst, device):
        return pltpu.make_async_remote_copy(
            src, dst, send.at[slot], recv.at[slot], device_id=device, device_id_type=MESH
        )

    def wide(ref):
        return ref[...].astype(jnp.float32)

    greet((to_pair, to_left, to_right) if mask else (to_left, to_right))
    far_ones, near_ones, added_ones, back = {}, {}, {}, {}
    for chunk in ORDER:
        device = to_left if chunk < 2 else to_right
        far_ones[chunk] = copy(chunk, part_ref.at[rows(far, chunk)], relay.at[rows(0, chunk)], device)
        far_ones[chunk].start()
    for chunk in ORDER:
        owner, place, device = (right, 0, to_right) if chunk < 2 else (left, 1, to_left)
        near_ones[chunk] = copy(
            4 + chunk, part_ref.at[rows(owner, chunk)], side.at[rows(place, chunk)], device
        )
        near_ones[chunk].start()
    for chunk in ORDER:
        owner, place, device = (left, 1, to_left) if chunk < 2 else (right, 0, to_right)
        far_ones[chunk].wait_recv()
        added[rows(0, chunk), :] = (
            wide(relay.at[rows(0, chunk)]) + wide(part_ref.at[rows(owner, chunk)])
        ).astype(jnp.bfloat16)
        added_ones[chunk] = copy(
            8 + chunk, added.at[rows(0, chunk)], side.at[rows(place, chunk)], device
        )
        added_ones[chunk].start()
    for chunk in ORDER:
        near_ones[chunk].wait_recv()
        added_ones[chunk].wait_recv()
        (total if mask else got)[rows(0, chunk), :] = (
            wide(part_ref.at[rows(me, chunk)])
            + wide(side.at[rows(0, chunk)])
            + wide(side.at[rows(1, chunk)])
        ).astype(jnp.bfloat16)
        if mask:
            back[chunk] = copy(12 + chunk, total.at[rows(0, chunk)], got.at[rows(0, chunk)], to_pair)
            back[chunk].start()
    for group in (far_ones, near_ones, added_ones, back):
        for sent in group.values():
            sent.wait_send()
    for sent in back.values():
        sent.wait_recv()


def reduced(mask, collective_id, dst_part):
    vmem = pl.BlockSpec(memory_space=pltpu.VMEM)
    low = jnp.bfloat16
    return pl.pallas_call(
        functools.partial(reduce_kernel, mask),
        out_shape=jax.ShapeDtypeStruct((TILE, D), low),
        in_specs=[vmem],
        out_specs=vmem,
        scratch_shapes=[
            pltpu.VMEM((TILE, D), low),
            pltpu.VMEM((TILE, D), low),
            pltpu.VMEM((2 * TILE, D), low),
            pltpu.VMEM((TILE, D), low),
            pltpu.SemaphoreType.DMA((16,)),
            pltpu.SemaphoreType.DMA((16,)),
        ],
        compiler_params=pltpu.CompilerParams(
            collective_id=collective_id, has_side_effects=True, vmem_limit_bytes=16 * 2**20
        ),
    )(dst_part)


def permute_kernel(mask, rows_ref, moved_ref, send, recv):
    to_pair = {"bucket": paired(mask)}
    greet((to_pair,))
    copy = pltpu.make_async_remote_copy(
        rows_ref, moved_ref, send, recv, device_id=to_pair, device_id_type=MESH
    )
    copy.start()
    copy.wait()


def permuted(mask, collective_id, block):
    if not mask:
        return block
    vmem = pl.BlockSpec(memory_space=pltpu.VMEM)
    return pl.pallas_call(
        functools.partial(permute_kernel, mask),
        out_shape=jax.ShapeDtypeStruct(block.shape, block.dtype),
        in_specs=[vmem],
        out_specs=vmem,
        scratch_shapes=[pltpu.SemaphoreType.DMA, pltpu.SemaphoreType.DMA],
        compiler_params=pltpu.CompilerParams(
            collective_id=collective_id, has_side_effects=True, vmem_limit_bytes=16 * 2**20
        ),
    )(block)


def adagrad_kernel(table_ref, state_ref, grad_ref, table_out, state_out, low_out):
    table_out[...], state_out[...] = adagrad_block(
        table_ref[...], state_ref[...], grad_ref[...].astype(jnp.float32), diagonal()
    )
    low_out[...] = table_out[...].astype(jnp.bfloat16)


def updated(table, state, grad):
    vmem = pl.BlockSpec(memory_space=pltpu.VMEM)
    return pl.pallas_call(
        adagrad_kernel,
        out_shape=(
            jax.ShapeDtypeStruct(table.shape, jnp.float32),
            jax.ShapeDtypeStruct(state.shape, jnp.float32),
            jax.ShapeDtypeStruct(grad.shape, jnp.bfloat16),
        ),
        in_specs=[vmem] * 3,
        out_specs=(vmem,) * 3,
        compiler_params=pltpu.CompilerParams(vmem_limit_bytes=16 * 2**20),
    )(table, state, grad)


Y_MASKS = tuple(y << 2 for y in range(8))
OTHER_MASKS = tuple((x << 5) + low for x in range(4) for low in range(4))


def along_y(make, first_id, index, block):
    branches = [functools.partial(make, mask, first_id + i) for i, mask in enumerate(Y_MASKS)]
    return lax.switch(index, branches, block)


def along_others(index, block):
    branches = [functools.partial(permuted, mask, i) for i, mask in enumerate(OTHER_MASKS)]
    return lax.switch(index, branches, block)


def prepare_kernel(
    partners_hbm, table_hbm, state_hbm, low_ref, table_ref, state_ref, *rest
):
    *index_refs, partners_ref, done = rest
    copies = [
        pltpu.make_async_copy(src, dst, done.at[i])
        for i, (src, dst) in enumerate(
            ((partners_hbm, partners_ref), (table_hbm, table_ref), (state_hbm, state_ref))
        )
    ]
    for copy in copies:
        copy.start()
    copies[0].wait()
    for round_index in range(ROUNDS):
        mask = partners_ref[round_index, 0]
        index_refs[2 * round_index][0, 0] = (mask >> 5) * 4 + (mask & 3)
        index_refs[2 * round_index + 1][0, 0] = (mask >> 2) & 7
    copies[1].wait()
    low_ref[...] = table_ref[...].astype(jnp.bfloat16)
    copies[2].wait()


def prepared(partners, table, state):
    smem = pl.BlockSpec(memory_space=pltpu.SMEM)
    vmem = pl.BlockSpec(memory_space=pltpu.VMEM)
    low, table, state, *indices = pl.pallas_call(
        prepare_kernel,
        out_shape=(
            jax.ShapeDtypeStruct(table.shape, jnp.bfloat16),
            jax.ShapeDtypeStruct(table.shape, jnp.float32),
            jax.ShapeDtypeStruct(state.shape, jnp.float32),
            *[jax.ShapeDtypeStruct((1, 1), jnp.int32)] * (2 * ROUNDS),
        ),
        in_specs=[pl.BlockSpec(memory_space=pltpu.HBM)] * 3,
        out_specs=(vmem, vmem, vmem, *[smem] * (2 * ROUNDS)),
        scratch_shapes=[
            pltpu.SMEM(partners.shape, jnp.int32),
            pltpu.SemaphoreType.DMA((3,)),
        ],
        compiler_params=pltpu.CompilerParams(vmem_limit_bytes=16 * 2**20),
    )(partners, table, state)
    return low, table, state, [index[0, 0] for index in indices]


UNROLL = 16


def tile_kernel(
    round_index, code_hbm, rel_id_hbm, count_hbm, src_ref, part_ref, rel_ref, state_ref,
    table_out, state_out, dst_out, src_low, src_grad, dst_grad, code_ref, rel_id_ref, count_ref, done
):
    copies = [
        pltpu.make_async_copy(src, dst, done.at[i])
        for i, (src, dst) in enumerate(
            ((code_hbm, code_ref), (rel_id_hbm, rel_id_ref), (count_hbm, count_ref))
        )
    ]
    for copy in copies:
        copy.start()
    src_low[...] = src_ref[...].astype(jnp.bfloat16).astype(jnp.float32)
    src_grad[...] = jnp.zeros_like(src_grad)
    dst_grad[...] = jnp.zeros_like(dst_grad)
    for copy in copies:
        copy.wait()
    live = count_ref[0, 0, round_index]
    row = lax.broadcasted_iota(jnp.int32, (TILE, TILE), 0)
    col = lax.broadcasted_iota(jnp.int32, (TILE, TILE), 1)
    shift = jnp.where(row == col, -0.5, 0.5).astype(jnp.float32)

    def step(group, carry):
        lanes = range(UNROLL)
        slots = [group * UNROLL + lane for lane in lanes]
        codes = [code_ref[0, 0, round_index, slot] for slot in slots]
        src_at = [pl.ds(pl.multiple_of((code // 4) * TILE, TILE), TILE) for code in codes]
        dst_at = [pl.ds(pl.multiple_of((code % 4) * TILE, TILE), TILE) for code in codes]
        rels = [rel_ref[pl.ds(rel_id_ref[0, 0, round_index, slot], 1), :] for slot in slots]
        dsts = [part_ref[at, :] for at in dst_at]
        src_rels = [(src_low[src_at[lane], :] * rels[lane]).astype(jnp.bfloat16) for lane in lanes]
        scores = [
            lax.dot_general(
                src_rels[lane], dsts[lane], (((1,), (1,)), ((), ())), preferred_element_type=jnp.float32
            )
            for lane in lanes
        ]
        ons = [jnp.where(slot < live, 1.0, 0.0).astype(jnp.float32) for slot in slots]
        slopes = [
            ((jnp.tanh(scores[lane] * (0.5 * D**-0.5)) * 0.5 + shift) * ons[lane]).astype(jnp.bfloat16)
            for lane in lanes
        ]
        src_terms = [
            jnp.dot(slopes[lane], dsts[lane], preferred_element_type=jnp.float32) for lane in lanes
        ]
        dst_terms = [
            lax.dot_general(
                slopes[lane], src_rels[lane], (((0,), (0,)), ((), ())), preferred_element_type=jnp.float32
            )
            for lane in lanes
        ]
        for lane in lanes:
            src_grad[src_at[lane], :] += src_terms[lane] * rels[lane]
            dst_grad[dst_at[lane], :] += dst_terms[lane]
        return carry

    lax.fori_loop(0, (live + UNROLL - 1) // UNROLL, step, 0)
    diag = row == col
    for block in range(src_ref.shape[0] // TILE):
        at = slice(block * TILE, (block + 1) * TILE)
        table_out[at, :], state_out[block : block + 1, :] = adagrad_block(
            src_ref[at, :], state_ref[block : block + 1, :], src_grad[at, :] * D**-0.5, diag
        )
    dst_out[...] = (dst_grad[...] * D**-0.5).astype(jnp.bfloat16)


def tile_work(
    round_index, src_table, src_state, partition, tile_list, rel_list, live_count, rel_table
):
    vmem = pl.BlockSpec(memory_space=pltpu.VMEM)
    return pl.pallas_call(
        functools.partial(tile_kernel, round_index),
        out_shape=(
            jax.ShapeDtypeStruct(src_table.shape, jnp.float32),
            jax.ShapeDtypeStruct(src_state.shape, jnp.float32),
            jax.ShapeDtypeStruct(partition.shape, jnp.bfloat16),
        ),
        in_specs=[pl.BlockSpec(memory_space=pltpu.HBM)] * 3 + [vmem] * 4,
        out_specs=(vmem, vmem, vmem),
        scratch_shapes=[
            pltpu.VMEM(src_table.shape, jnp.float32),
            pltpu.VMEM(src_table.shape, jnp.float32),
            pltpu.VMEM(partition.shape, jnp.float32),
            pltpu.SMEM(tile_list.shape, jnp.int32),
            pltpu.SMEM(rel_list.shape, jnp.int32),
            pltpu.SMEM(live_count.shape, jnp.int32),
            pltpu.SemaphoreType.DMA((3,)),
        ],
        compiler_params=pltpu.CompilerParams(vmem_limit_bytes=32 * 2**20),
    )(tile_list, rel_list, live_count, src_table, partition, rel_table, src_state)


def per_device(
    src_table, src_state, dst_table, dst_state, rel_table, partners, tiles, tile_rel, counts
):
    src_state = src_state.reshape(-1, TILE)
    dst_state = dst_state.reshape(-1, TILE)
    low, dst_table, dst_state, indices = prepared(partners, dst_table, dst_state)
    for round_index in range(ROUNDS):
        others, y = indices[2 * round_index : 2 * round_index + 2]
        moved = along_others(others, low)
        partition = along_y(gathered, 16, y, moved)
        src_table, src_state, dst_part = tile_work(
            round_index, src_table, src_state, partition, tiles, tile_rel, counts, rel_table
        )
        summed = along_y(reduced, 24, y, dst_part)
        grad = along_others(others, summed)
        dst_table, dst_state, low = updated(dst_table, dst_state, grad)
    return (src_table, src_state.reshape(-1), dst_table, dst_state.reshape(-1))


def solution(mesh):
    in_specs = (
        P(("bucket", "rep"), None),
        P(("bucket", "rep")),
        P(("bucket", "rep"), None),
        P(("bucket", "rep")),
        P(),
        P(),
        P("bucket", "rep", None, None),
        P("bucket", "rep", None, None),
        P("bucket", "rep", None),
    )
    out_specs = (
        P(("bucket", "rep"), None),
        P(("bucket", "rep")),
        P(("bucket", "rep"), None),
        P(("bucket", "rep")),
    )
    return jax.shard_map(
        per_device, mesh=mesh, in_specs=in_specs, out_specs=out_specs, check_vma=False
    )
```

```python
import functools

import jax
import jax.numpy as jnp
from jax import lax
from jax.experimental import pallas as pl
from jax.experimental.pallas import tpu as pltpu
from jax.sharding import PartitionSpec as P

D = 256
TILE = 128
ROUNDS = 2


learn_rate = 0.1


CHUNK = TILE // 4
ORDER = (0, 2, 1, 3)
MESH = pl.DeviceIdType.MESH


def paired(mask):
    me = lax.axis_index("bucket")
    other = me
    for bit in range(mask.bit_length()):
        if mask >> bit & 1:
            other = other + (1 << bit) * (1 - 2 * lax.rem(lax.div(me, 1 << bit), 2))
    return other


def around():
    me = lax.axis_index("rep")
    return me, lax.rem(me + 3, 4), lax.rem(me + 1, 4), lax.rem(me + 2, 4)


def greet(devices):
    barrier = pltpu.get_barrier_semaphore()
    for device in devices:
        pl.semaphore_signal(barrier, inc=1, device_id=device, device_id_type=MESH)
    pl.semaphore_wait(barrier, len(devices))


def rows(quarter, chunk):
    return pl.ds(pl.multiple_of(quarter * TILE + chunk * CHUNK, CHUNK), CHUNK)


def gather_kernel(mask, low_ref, part_ref, send, recv):
    me, left, right, far = around()
    to_left, to_right, to_pair = {"rep": left}, {"rep": right}, {"bucket": paired(mask)}

    def copy(slot, src, dst, device):
        return pltpu.make_async_remote_copy(
            src, dst, send.at[slot], recv.at[slot], device_id=device, device_id_type=MESH
        )

    greet((to_pair, to_left, to_right) if mask else (to_left, to_right))
    own = [part_ref.at[rows(me, chunk)] for chunk in range(4)]
    hop = {}
    if mask:
        for chunk in ORDER:
            hop[chunk] = copy(chunk, low_ref.at[rows(0, chunk)], own[chunk], to_pair)
            hop[chunk].start()
    else:
        part_ref[pl.ds(pl.multiple_of(me * TILE, TILE), TILE), :] = low_ref[...]
    going_right = [copy(4 + chunk, own[chunk], own[chunk], to_right) for chunk in range(4)]
    going_left = [copy(8 + chunk, own[chunk], own[chunk], to_left) for chunk in range(4)]
    for chunk in ORDER:
        if mask:
            hop[chunk].wait_recv()
        near = (going_right, going_left) if chunk < 2 else (going_left, going_right)
        near[0][chunk].start()
        near[1][chunk].start()
    onward = []
    for chunk in ORDER:
        came, source, device = (
            (going_right, left, to_right) if chunk < 2 else (going_left, right, to_left)
        )
        came[chunk].wait_recv()
        passed = part_ref.at[rows(source, chunk)]
        onward.append(copy(12 + chunk, passed, passed, device))
        onward[-1].start()
    for sent in (*hop.values(), *going_right, *going_left):
        sent.wait_send()
    for chunk in range(4):
        (going_left if chunk < 2 else going_right)[chunk].wait_recv()
    for sent in onward:
        sent.wait_send()
    for passed in onward:
        passed.wait_recv()


def gathered(mask, collective_id, low):
    vmem = pl.BlockSpec(memory_space=pltpu.VMEM)
    return pl.pallas_call(
        functools.partial(gather_kernel, mask),
        out_shape=jax.ShapeDtypeStruct((4 * TILE, D), jnp.bfloat16),
        in_specs=[vmem],
        out_specs=vmem,
        scratch_shapes=[pltpu.SemaphoreType.DMA((16,)), pltpu.SemaphoreType.DMA((16,))],
        compiler_params=pltpu.CompilerParams(
            collective_id=collective_id, has_side_effects=True, vmem_limit_bytes=16 * 2**20
        ),
    )(low)


def diagonal():
    row = lax.broadcasted_iota(jnp.int32, (TILE, TILE), 0)
    col = lax.broadcasted_iota(jnp.int32, (TILE, TILE), 1)
    return row == col


def adagrad_block(table, state_row, grad, diag):
    mean = jnp.sum(grad * grad, axis=1, keepdims=True) * (1 / D)
    state = jnp.sum(jnp.where(diag, state_row, 0.0), axis=1, keepdims=True) + mean
    table = table - grad * (learn_rate / jnp.sqrt(state))
    return table, jnp.sum(jnp.where(diag, state, 0.0), axis=0, keepdims=True)


def reduce_kernel(
    mask, part_ref, got, relay, added, side, total, send, recv
):
    me, left, right, far = around()
    to_left, to_right, to_pair = {"rep": left}, {"rep": right}, {"bucket": paired(mask)}

    def copy(slot, src, dst, device):
        return pltpu.make_async_remote_copy(
            src, dst, send.at[slot], recv.at[slot], device_id=device, device_id_type=MESH
        )

    def wide(ref):
        return ref[...].astype(jnp.float32)

    greet((to_pair, to_left, to_right) if mask else (to_left, to_right))
    far_ones, near_ones, added_ones, back = {}, {}, {}, {}
    for chunk in ORDER:
        device = to_left if chunk < 2 else to_right
        far_ones[chunk] = copy(chunk, part_ref.at[rows(far, chunk)], relay.at[rows(0, chunk)], device)
        far_ones[chunk].start()
    for chunk in ORDER:
        owner, place, device = (right, 0, to_right) if chunk < 2 else (left, 1, to_left)
        near_ones[chunk] = copy(
            4 + chunk, part_ref.at[rows(owner, chunk)], side.at[rows(place, chunk)], device
        )
        near_ones[chunk].start()
    for chunk in ORDER:
        owner, place, device = (left, 1, to_left) if chunk < 2 else (right, 0, to_right)
        far_ones[chunk].wait_recv()
        added[rows(0, chunk), :] = (
            wide(relay.at[rows(0, chunk)]) + wide(part_ref.at[rows(owner, chunk)])
        ).astype(jnp.bfloat16)
        added_ones[chunk] = copy(
            8 + chunk, added.at[rows(0, chunk)], side.at[rows(place, chunk)], device
        )
        added_ones[chunk].start()
    for chunk in ORDER:
        near_ones[chunk].wait_recv()
        added_ones[chunk].wait_recv()
        (total if mask else got)[rows(0, chunk), :] = (
            wide(part_ref.at[rows(me, chunk)])
            + wide(side.at[rows(0, chunk)])
            + wide(side.at[rows(1, chunk)])
        ).astype(jnp.bfloat16)
        if mask:
            back[chunk] = copy(12 + chunk, total.at[rows(0, chunk)], got.at[rows(0, chunk)], to_pair)
            back[chunk].start()
    for group in (far_ones, near_ones, added_ones, back):
        for sent in group.values():
            sent.wait_send()
    for sent in back.values():
        sent.wait_recv()


def reduced(mask, collective_id, dst_part):
    vmem = pl.BlockSpec(memory_space=pltpu.VMEM)
    low = jnp.bfloat16
    return pl.pallas_call(
        functools.partial(reduce_kernel, mask),
        out_shape=jax.ShapeDtypeStruct((TILE, D), low),
        in_specs=[vmem],
        out_specs=vmem,
        scratch_shapes=[
            pltpu.VMEM((TILE, D), low),
            pltpu.VMEM((TILE, D), low),
            pltpu.VMEM((2 * TILE, D), low),
            pltpu.VMEM((TILE, D), low),
            pltpu.SemaphoreType.DMA((16,)),
            pltpu.SemaphoreType.DMA((16,)),
        ],
        compiler_params=pltpu.CompilerParams(
            collective_id=collective_id, has_side_effects=True, vmem_limit_bytes=16 * 2**20
        ),
    )(dst_part)


def permute_kernel(mask, rows_ref, moved_ref, send, recv):
    to_pair = {"bucket": paired(mask)}
    greet((to_pair,))
    copy = pltpu.make_async_remote_copy(
        rows_ref, moved_ref, send, recv, device_id=to_pair, device_id_type=MESH
    )
    copy.start()
    copy.wait()


def permuted(mask, collective_id, block):
    if not mask:
        return block
    vmem = pl.BlockSpec(memory_space=pltpu.VMEM)
    return pl.pallas_call(
        functools.partial(permute_kernel, mask),
        out_shape=jax.ShapeDtypeStruct(block.shape, block.dtype),
        in_specs=[vmem],
        out_specs=vmem,
        scratch_shapes=[pltpu.SemaphoreType.DMA, pltpu.SemaphoreType.DMA],
        compiler_params=pltpu.CompilerParams(
            collective_id=collective_id, has_side_effects=True, vmem_limit_bytes=16 * 2**20
        ),
    )(block)


def adagrad_kernel(table_ref, state_ref, grad_ref, table_out, state_out, *low_out):
    table_out[...], state_out[...] = adagrad_block(
        table_ref[...], state_ref[...], grad_ref[...].astype(jnp.float32), diagonal()
    )
    for low in low_out:
        low[...] = table_out[...].astype(jnp.bfloat16)


def updated(table, state, grad, last):
    vmem = pl.BlockSpec(memory_space=pltpu.VMEM)
    outs = (
        jax.ShapeDtypeStruct(table.shape, jnp.float32),
        jax.ShapeDtypeStruct(state.shape, jnp.float32),
        jax.ShapeDtypeStruct(grad.shape, jnp.bfloat16),
    )[: 2 if last else 3]
    return pl.pallas_call(
        adagrad_kernel,
        out_shape=outs,
        in_specs=[vmem] * 3,
        out_specs=(vmem,) * len(outs),
        compiler_params=pltpu.CompilerParams(vmem_limit_bytes=16 * 2**20),
    )(table, state, grad)


Y_MASKS = tuple(y << 2 for y in range(8))
OTHER_MASKS = tuple((x << 5) + low for x in range(4) for low in range(4))


def along_y(make, first_id, index, block):
    branches = [functools.partial(make, mask, first_id + i) for i, mask in enumerate(Y_MASKS)]
    return lax.switch(index, branches, block)


def along_others(index, block):
    branches = [functools.partial(permuted, mask, i) for i, mask in enumerate(OTHER_MASKS)]
    return lax.switch(index, branches, block)


def prepare_kernel(
    partners_hbm, table_hbm, state_hbm, low_ref, table_ref, state_ref, *rest
):
    *index_refs, partners_ref, done = rest
    copies = [
        pltpu.make_async_copy(src, dst, done.at[i])
        for i, (src, dst) in enumerate(
            ((partners_hbm, partners_ref), (table_hbm, table_ref), (state_hbm, state_ref))
        )
    ]
    for copy in copies:
        copy.start()
    copies[0].wait()
    for round_index in range(ROUNDS):
        mask = partners_ref[round_index, 0]
        index_refs[2 * round_index][0, 0] = (mask >> 5) * 4 + (mask & 3)
        index_refs[2 * round_index + 1][0, 0] = (mask >> 2) & 7
    copies[1].wait()
    low_ref[...] = table_ref[...].astype(jnp.bfloat16)
    copies[2].wait()


def prepared(partners, table, state):
    smem = pl.BlockSpec(memory_space=pltpu.SMEM)
    vmem = pl.BlockSpec(memory_space=pltpu.VMEM)
    low, table, state, *indices = pl.pallas_call(
        prepare_kernel,
        out_shape=(
            jax.ShapeDtypeStruct(table.shape, jnp.bfloat16),
            jax.ShapeDtypeStruct(table.shape, jnp.float32),
            jax.ShapeDtypeStruct(state.shape, jnp.float32),
            *[jax.ShapeDtypeStruct((1, 1), jnp.int32)] * (2 * ROUNDS),
        ),
        in_specs=[pl.BlockSpec(memory_space=pltpu.HBM)] * 3,
        out_specs=(vmem, vmem, vmem, *[smem] * (2 * ROUNDS)),
        scratch_shapes=[
            pltpu.SMEM(partners.shape, jnp.int32),
            pltpu.SemaphoreType.DMA((3,)),
        ],
        compiler_params=pltpu.CompilerParams(vmem_limit_bytes=16 * 2**20),
    )(partners, table, state)
    return low, table, state, [index[0, 0] for index in indices]


UNROLL = 32


def tile_kernel(
    round_index, code_hbm, rel_id_hbm, count_hbm, src_ref, part_ref, rel_ref, state_ref,
    table_out, state_out, dst_out, src_low, src_grad, dst_grad, code_ref, rel_id_ref, count_ref, done
):
    copies = [
        pltpu.make_async_copy(src, dst, done.at[i])
        for i, (src, dst) in enumerate(
            ((code_hbm, code_ref), (rel_id_hbm, rel_id_ref), (count_hbm, count_ref))
        )
    ]
    for copy in copies:
        copy.start()
    src_low[...] = src_ref[...].astype(jnp.bfloat16).astype(jnp.float32)
    src_grad[...] = jnp.zeros_like(src_grad)
    dst_grad[...] = jnp.zeros_like(dst_grad)
    for copy in copies:
        copy.wait()
    live = count_ref[0, 0, round_index]
    row = lax.broadcasted_iota(jnp.int32, (TILE, TILE), 0)
    col = lax.broadcasted_iota(jnp.int32, (TILE, TILE), 1)
    shift = jnp.where(row == col, -0.5, 0.5).astype(jnp.float32)

    def step(group, carry):
        lanes = range(UNROLL)
        slots = [group * UNROLL + lane for lane in lanes]
        codes = [code_ref[0, 0, round_index, slot] for slot in slots]
        src_at = [pl.ds(pl.multiple_of((code // 4) * TILE, TILE), TILE) for code in codes]
        dst_at = [pl.ds(pl.multiple_of((code % 4) * TILE, TILE), TILE) for code in codes]
        rels = [rel_ref[pl.ds(rel_id_ref[0, 0, round_index, slot], 1), :] for slot in slots]
        dsts = [part_ref[at, :] for at in dst_at]
        src_rels = [(src_low[src_at[lane], :] * rels[lane]).astype(jnp.bfloat16) for lane in lanes]
        scores = [
            lax.dot_general(
                src_rels[lane], dsts[lane], (((1,), (1,)), ((), ())), preferred_element_type=jnp.float32
            )
            for lane in lanes
        ]
        ons = [jnp.where(slot < live, 1.0, 0.0).astype(jnp.float32) for slot in slots]
        slopes = [
            ((jnp.tanh(scores[lane] * (0.5 * D**-0.5)) * 0.5 + shift) * ons[lane]).astype(jnp.bfloat16)
            for lane in lanes
        ]
        src_terms = [
            jnp.dot(slopes[lane], dsts[lane], preferred_element_type=jnp.float32) for lane in lanes
        ]
        dst_terms = [
            lax.dot_general(
                slopes[lane], src_rels[lane], (((0,), (0,)), ((), ())), preferred_element_type=jnp.float32
            )
            for lane in lanes
        ]
        for lane in lanes:
            src_grad[src_at[lane], :] += src_terms[lane] * rels[lane]
            dst_grad[dst_at[lane], :] += dst_terms[lane]
        return carry

    lax.fori_loop(0, (live + UNROLL - 1) // UNROLL, step, 0)
    diag = row == col
    for block in range(src_ref.shape[0] // TILE):
        at = slice(block * TILE, (block + 1) * TILE)
        table_out[at, :], state_out[block : block + 1, :] = adagrad_block(
            src_ref[at, :], state_ref[block : block + 1, :], src_grad[at, :] * D**-0.5, diag
        )
    dst_out[...] = (dst_grad[...] * D**-0.5).astype(jnp.bfloat16)


def tile_work(
    round_index, src_table, src_state, partition, tile_list, rel_list, live_count, rel_table
):
    vmem = pl.BlockSpec(memory_space=pltpu.VMEM)
    return pl.pallas_call(
        functools.partial(tile_kernel, round_index),
        out_shape=(
            jax.ShapeDtypeStruct(src_table.shape, jnp.float32),
            jax.ShapeDtypeStruct(src_state.shape, jnp.float32),
            jax.ShapeDtypeStruct(partition.shape, jnp.bfloat16),
        ),
        in_specs=[pl.BlockSpec(memory_space=pltpu.HBM)] * 3 + [vmem] * 4,
        out_specs=(vmem, vmem, vmem),
        scratch_shapes=[
            pltpu.VMEM(src_table.shape, jnp.float32),
            pltpu.VMEM(src_table.shape, jnp.float32),
            pltpu.VMEM(partition.shape, jnp.float32),
            pltpu.SMEM(tile_list.shape, jnp.int32),
            pltpu.SMEM(rel_list.shape, jnp.int32),
            pltpu.SMEM(live_count.shape, jnp.int32),
            pltpu.SemaphoreType.DMA((3,)),
        ],
        compiler_params=pltpu.CompilerParams(vmem_limit_bytes=32 * 2**20),
    )(tile_list, rel_list, live_count, src_table, partition, rel_table, src_state)


def per_device(
    src_table, src_state, dst_table, dst_state, rel_table, partners, tiles, tile_rel, counts
):
    src_state = src_state.reshape(-1, TILE)
    dst_state = dst_state.reshape(-1, TILE)
    *low, dst_table, dst_state, indices = prepared(partners, dst_table, dst_state)
    for round_index in range(ROUNDS):
        others, y = indices[2 * round_index : 2 * round_index + 2]
        moved = along_others(others, *low)
        partition = along_y(gathered, 16, y, moved)
        src_table, src_state, dst_part = tile_work(
            round_index, src_table, src_state, partition, tiles, tile_rel, counts, rel_table
        )
        summed = along_y(reduced, 24, y, dst_part)
        grad = along_others(others, summed)
        last = round_index == ROUNDS - 1
        dst_table, dst_state, *low = updated(dst_table, dst_state, grad, last)
    return (src_table, src_state.reshape(-1), dst_table, dst_state.reshape(-1))


def solution(mesh):
    in_specs = (
        P(("bucket", "rep"), None),
        P(("bucket", "rep")),
        P(("bucket", "rep"), None),
        P(("bucket", "rep")),
        P(),
        P(),
        P("bucket", "rep", None, None),
        P("bucket", "rep", None, None),
        P("bucket", "rep", None),
    )
    out_specs = (
        P(("bucket", "rep"), None),
        P(("bucket", "rep")),
        P(("bucket", "rep"), None),
        P(("bucket", "rep")),
    )
    return jax.shard_map(
        per_device, mesh=mesh, in_specs=in_specs, out_specs=out_specs, check_vma=False
    )
```
